32 devices in a mesh: grp: 1, wide: 8 (over z, y), narrow: 4 (over x, core).
Axes of the slice: x: 2, y: 2, z: 4, core: 2. Of those that a mesh axis runs over, the one named last changes fastest.
Arguments:
- vectors: bfloat16 [512, 2, 3, 16, 512], P('grp', None, None, 'wide', 'narrow'), may hold values from -6 to 6
- links: float32 [3, 2, 3, 3, 16, 512], P('grp', None, None, None, 'wide', 'narrow'), may hold values from -4 to 4
- directions: int32 [3], replicated, may hold values from 0 to 2, each once
- peram: bfloat16 [2, 512, 256], P('grp', 'wide', 'narrow'), may hold values from -0.1875 to 0.1875
Outputs:
- elementals: float32 [3, 2, 512, 512], P('grp', None, 'wide')
- products: float32 [3, 2, 512, 256], P('grp', None, 'wide', 'narrow')
The draws below stay inside these ranges and needn't reach their ends.
All inputs are finite; a program needn't handle non-finite values.
Results may differ from the reference program's by a relative error of at most 0.004.
Values may be sent and summed in bfloat16 or wider, within the bound.
No kernel may reach another device: no remote copies, remote signals or barrier semaphores. Data moves between devices by JAX's collectives and lax.ppermute only.
A program may use at most 64 MiB of HBM per device.

```python
import math
import jax
import jax.numpy as jnp
from jax import lax

NVEC = 512
NCOL = 256
NDIR = 3
NX = 16
NY = 32
NZ = 16


def level_of(key, dims, pieces, least, largest):
    gain = 1.0
    for dim, parts in pieces:
        draws = jax.random.uniform(jax.random.fold_in(jax.random.fold_in(key, 6), dim), (parts,), jnp.float32, least / len(pieces), largest / len(pieces))
        gain = gain * jnp.repeat(jnp.exp(draws), dims[dim] // parts).reshape((-1,) + (1,) * (len(dims) - 1 - dim))
    return gain


def centred(key, dims, deviation, bound, shards=(), held_as=jnp.bfloat16):
    result = deviation * jax.random.normal(key, dims, jnp.float32)
    if shards:
        result = result * level_of(key, dims, shards, -0.22, 0.18)
    return jnp.clip(result, -bound, bound).astype(held_as)


def setup_inputs(seed: int = 0, part: int = 0) -> dict:
    streams_of = jax.random.split(jax.random.key(seed), 5)
    part_keys = jax.random.split(jax.random.fold_in(streams_of[4], part), 5)
    return {
        "vectors": centred(part_keys[0], (NVEC, 2, 3, NX, NY * NZ), 1.0, 6.0, ((3, 8), (4, 4))),
        "links": centred(part_keys[1], (3, 2, 3, 3, NX, NY * NZ), 0.577, 4.0, ((4, 8), (5, 4)), jnp.float32),
        "directions": jax.random.permutation(streams_of[2], NDIR).astype(jnp.int32),
        "peram": centred(part_keys[3], (2, NVEC, NCOL), (2 * NVEC) ** -0.5, 0.1875, ((1, 8), (2, 4))),
    }


def covariant_product(link_field, shifted):
    link_real = link_field[0][None]
    link_imag = link_field[1][None]
    vec_real = shifted[:, 0][:, None]
    vec_imag = shifted[:, 1][:, None]
    out_real = lax.optimization_barrier(jnp.sum(link_real * vec_real - link_imag * vec_imag, axis=2))
    out_imag = lax.optimization_barrier(jnp.sum(link_real * vec_imag + link_imag * vec_real, axis=2))
    return jnp.stack([out_real, out_imag], 1).astype(jnp.bfloat16)

def reference(vectors, links, directions, peram):
    vec_count = vectors.shape[0]
    col_count = peram.shape[2]
    norm_factor = 1.0 / math.sqrt(12.0 * NX * NY * NZ)

    def plane_step(carry, position):
        plane = lax.dynamic_index_in_dim(vectors, position, 3, keepdims=False)
        ahead = lax.dynamic_index_in_dim(vectors, (position + 1) % NX, 3, keepdims=False)
        link_plane = lax.dynamic_index_in_dim(links, position, 4, keepdims=False)
        along_second = jnp.roll(plane, -NZ, axis=3)
        along_third = jnp.roll(plane.reshape(vec_count, 2, 3, NY, NZ), -1, axis=4).reshape(plane.shape)
        rotated = jnp.concatenate([-plane[:, 1:2], plane[:, 0:1]], 1)
        left_block = jnp.concatenate([plane.reshape(vec_count, -1), rotated.reshape(vec_count, -1)], 0)
        partials = []
        for slot_index in range(NDIR):
            chosen = directions[slot_index]
            shifted = jnp.where(chosen == 0, ahead, jnp.where(chosen == 1, along_second, along_third))
            link_field = jnp.where(chosen == 0, link_plane[0], jnp.where(chosen == 1, link_plane[1], link_plane[2]))
            product = covariant_product(link_field, shifted).reshape(vec_count, -1)
            partials.append(jnp.dot(left_block, product.T, preferred_element_type=jnp.float32))
        return (carry + jnp.stack(partials), None)
    initial = jnp.zeros((NDIR, 2 * vec_count, vec_count), jnp.float32)
    total, _ = lax.scan(plane_step, initial, jnp.arange(NX, dtype=jnp.int32))
    halves = total.reshape(NDIR, 2, vec_count, vec_count) * norm_factor
    real_part = halves[:, 0]
    imag_part = halves[:, 1]
    elementals = jnp.stack([real_part - jnp.swapaxes(real_part, 1, 2), imag_part + jnp.swapaxes(imag_part, 1, 2)], 1)
    elem_low = elementals.astype(jnp.bfloat16)
    left_rows = jnp.concatenate([elem_low[:, 0], elem_low[:, 1]], 2).reshape(NDIR * vec_count, 2 * vec_count)
    peram_real = peram[0]
    peram_imag = peram[1]
    right_block = jnp.concatenate([jnp.concatenate([peram_real, peram_imag], 1), jnp.concatenate([-peram_imag, peram_real], 1)], 0)
    summed = jnp.dot(left_rows, right_block, preferred_element_type=jnp.float32)
    products = summed.reshape(NDIR, vec_count, 2, col_count).transpose(0, 2, 1, 3)
    return (elementals, products)
```

```python
import functools
import math

import jax
import jax.numpy as jnp
from jax import lax
from jax.experimental import pallas as pl
from jax.experimental.pallas import tpu as pltpu
from jax.sharding import PartitionSpec as P

LZ = 16
COMP = 6
VMEM_BYTES = 40 * 1024 * 1024
FLOAT = jnp.float32
SHORT = jnp.bfloat16

VMEM_SPEC = pl.BlockSpec(memory_space=pltpu.VMEM)
SMEM_SPEC = pl.BlockSpec(memory_space=pltpu.SMEM)


def call(kernel, out_shape, in_specs, scratch=(), flops=0, size=0):
    return pl.pallas_call(
        kernel,
        out_shape=out_shape,
        in_specs=in_specs,
        out_specs=jax.tree.map(lambda _: VMEM_SPEC, out_shape),
        scratch_shapes=list(scratch),
        compiler_params=pltpu.CompilerParams(vmem_limit_bytes=VMEM_BYTES),
        cost_estimate=pl.CostEstimate(flops=flops, bytes_accessed=size, transcendentals=0),
    )


def from_behind(x, axis, by):
    length = lax.axis_size(axis)
    return lax.ppermute(x, axis, [(i, (i + by) % length) for i in range(length)])


def swap(x, axis, mask):
    length = lax.axis_size(axis)
    return lax.ppermute(x, axis, [(i, i ^ mask) for i in range(length)])


def split_kernel(planes, x_ref, all_ref, first_ref, edge_ref, wide_scr):
    count = all_ref.shape[0]
    length = x_ref.shape[1]
    per_tile = length // LZ
    wide_scr[...] = x_ref[...].astype(FLOAT)
    lane = lax.broadcasted_iota(jnp.int32, (count, length), 1)
    tiles = [jnp.zeros((count, length), FLOAT)] * (edge_ref.shape[1] // length)
    for plane in range(planes):
        for comp in range(COMP):
            values = wide_scr[pl.ds(comp * planes + plane, count, stride=COMP * planes), :]
            low = values.astype(SHORT)
            at = (plane * COMP + comp) * length
            all_ref[:, at : at + length] = low
            if plane == 0:
                first_ref[:, comp * length : (comp + 1) * length] = low
            tile, slot = divmod(plane * COMP + comp, per_tile)
            moved = values if slot == 0 else pltpu.roll(values, slot * LZ, 1)
            tiles[tile] = jnp.where(lane // LZ == slot, moved, tiles[tile])
    for tile, values in enumerate(tiles):
        edge_ref[:, tile * length : (tile + 1) * length] = values.astype(SHORT)


def split_vectors(vectors):
    count, _, _, planes, length = vectors.shape
    rows = COMP * planes
    edge_tiles = -(-rows // (length // LZ))
    block = 64
    shapes = [rows * length, COMP * length, edge_tiles * length]
    return pl.pallas_call(
        functools.partial(split_kernel, planes),
        grid=(count // block,),
        out_shape=[jax.ShapeDtypeStruct((count, s), SHORT) for s in shapes],
        in_specs=[pl.BlockSpec((block * rows, length), lambda i: (i, 0))],
        out_specs=[pl.BlockSpec((block, s), lambda i: (i, 0)) for s in shapes],
        scratch_shapes=[pltpu.VMEM((block * rows, length), FLOAT)],
        compiler_params=pltpu.CompilerParams(vmem_limit_bytes=VMEM_BYTES),
    )(vectors.reshape(count * rows, length))


def times_transposed(left, right):
    return lax.dot_general(left, right, (((1,), (1,)), ((), ())), preferred_element_type=FLOAT)


def direction_kernel(direction, chosen, planes, norm, has_more, has_halo, *refs):
    here_ref, links_ref, vec_ref = refs[:3]
    rest = list(refs[3:])
    halo_ref = rest.pop(0) if has_halo else None
    more_ref = rest.pop(0) if has_more is True else None
    if has_more == "first":
        whole_ref, fwd_scr, rot_scr = rest
        packed = whole_ref
    else:
        keep_ref, send_ref, fwd_scr, rot_scr, packed = rest
    count = vec_ref.shape[0]
    length = links_ref.shape[1]
    part = 3 * length
    per_tile = length // LZ
    group = 16
    lane = lax.broadcasted_iota(jnp.int32, (group, length), 1)

    def ahead(rows, plane, comp):
        at = (plane * COMP + comp) * length
        if direction == 0:
            if plane + 1 < planes:
                return vec_ref[rows, at + COMP * length : at + (COMP + 1) * length].astype(FLOAT)
            return halo_ref[rows, comp * length : (comp + 1) * length].astype(FLOAT)
        values = vec_ref[rows, at : at + length].astype(FLOAT)
        if direction == 1:
            tile, slot = divmod(plane * COMP + comp, per_tile)
            edge = halo_ref[rows, tile * length : (tile + 1) * length].astype(FLOAT)
            shift = length - LZ - slot * LZ
            edge = edge if shift == 0 else pltpu.roll(edge, shift, 1)
            return jnp.where(lane < length - LZ, pltpu.roll(values, length - LZ, 1), edge)
        return jnp.where(
            lane % LZ == LZ - 1, pltpu.roll(values, LZ - 1, 1), pltpu.roll(values, length - 1, 1)
        )

    for position, plane in enumerate(chosen):
        base = position * COMP * length

        def link(r, a, b):
            row = (((direction * 2 + r) * 3 + a) * 3 + b) * planes + plane
            return links_ref[row : row + 1, :]

        matrix = [[[link(r, a, b) for b in range(3)] for a in range(3)] for r in range(2)]

        def step(index, carry):
            rows = pl.ds(pl.multiple_of(index * group, group), group)
            real = [ahead(rows, plane, b) for b in range(3)]
            imag = [ahead(rows, plane, 3 + b) for b in range(3)]
            for a in range(3):
                out_real = sum(
                    matrix[0][a][b] * real[b] - matrix[1][a][b] * imag[b] for b in range(3)
                )
                out_imag = sum(
                    matrix[0][a][b] * imag[b] + matrix[1][a][b] * real[b] for b in range(3)
                )
                low_real = out_real.astype(SHORT)
                low_imag = out_imag.astype(SHORT)
                at = base + a * length
                fwd_scr[rows, at : at + length] = low_real
                fwd_scr[rows, at + part : at + part + length] = low_imag
                rot_scr[rows, at : at + length] = low_imag
                rot_scr[rows, at + part : at + part + length] = -low_real
            return carry

        lax.fori_loop(0, count // group, step, 0)

    here = here_ref[0]
    pieces = packed.shape[0]
    size = packed.shape[2]
    tile = min(256, count)
    first = chosen[0] * COMP * length
    depth = len(chosen) * COMP * length
    row = lax.broadcasted_iota(jnp.int32, (tile, tile), 0)
    col = lax.broadcasted_iota(jnp.int32, (tile, tile), 1)

    def vec(i):
        return vec_ref[i * tile : (i + 1) * tile, first : first + depth]

    def fwd(i):
        return fwd_scr[i * tile : (i + 1) * tile, :]

    def rot(i):
        return rot_scr[i * tile : (i + 1) * tile, :]

    for i in range(count // tile):
        for j in range(count // tile):
            if i < j:
                value = times_transposed(vec(i), fwd(j)) - times_transposed(fwd(i), vec(j))
            elif i > j:
                value = times_transposed(vec(i), rot(j)) + times_transposed(rot(i), vec(j))
            else:
                real = times_transposed(vec(i), fwd(i))
                imag = times_transposed(vec(i), rot(i))
                other = jnp.where(row > col, -real, imag)
                value = jnp.where(row < col, real, imag) + other.T
            value = value * norm
            for p in range(tile // size):
                for q in range(tile // size):
                    block_row = i * (tile // size) + p
                    block_col = j * (tile // size) + q
                    slot = here ^ (block_row ^ block_col)
                    block = value[p * size : (p + 1) * size, q * size : (q + 1) * size]
                    if more_ref is not None:
                        block = block + more_ref[slot, block_row]
                    packed[slot, block_row] = block
    if has_more != "first":
        for piece in range(pieces // 2):
            keep_ref[piece] = packed[2 * piece]
            send_ref[piece] = packed[2 * piece + 1].astype(SHORT)


def direction_part(direction, chosen, norm, pieces, here, links, vec, halo=None, more=None):
    planes = vec.shape[1] // (COMP * links.shape[1])
    count = vec.shape[0]
    size = count // pieces
    depth = len(chosen) * COMP * links.shape[1]
    whole = jax.ShapeDtypeStruct((pieces, pieces, size, size), FLOAT)
    if more == "first":
        out_shape = whole
    else:
        half = (pieces // 2, pieces, size, size)
        out_shape = [jax.ShapeDtypeStruct(half, FLOAT), jax.ShapeDtypeStruct(half, SHORT)]
    scratch = [pltpu.VMEM((count, depth), SHORT)] * 2
    if more != "first":
        scratch.append(pltpu.VMEM(whole.shape, FLOAT))
    operands = [here, links, vec]
    if halo is not None:
        operands.append(halo)
    has_more = more if more == "first" else more is not None
    if has_more is True:
        operands.append(more)
    return call(
        functools.partial(
            direction_kernel, direction, chosen, planes, norm, has_more, halo is not None
        ),
        out_shape,
        [SMEM_SPEC] + [VMEM_SPEC] * (len(operands) - 1),
        scratch,
        flops=4 * count * count * depth,
        size=8 * count * depth,
    )(*operands)


def expand_kernel(here_ref, keep_ref, came_ref, own_ref, *rest):
    send_refs, sum_scr, rows_scr = rest[:-2], rest[-2], rest[-1]
    narrow, wide = here_ref[0], here_ref[1]
    kinds, pieces, size, _ = keep_ref.shape
    rows = own_ref.shape[2]
    per_block = size // rows
    row = lax.broadcasted_iota(jnp.int32, (size, size), 0)
    col = lax.broadcasted_iota(jnp.int32, (size, size), 1)
    sum_scr[...] = keep_ref[...] + came_ref[...].astype(FLOAT)
    for kind in range(kinds):
        for block in range(pieces):
            across = narrow ^ block
            mine = sum_scr[kind, block]
            other = sum_scr[kind, across].T
            ahead = row + block * size - col - across * size
            real = jnp.where(ahead < 0, mine, jnp.where(ahead > 0, -other, 0.0))
            imag = jnp.where(ahead < 0, other, mine)
            for part in range(per_block):
                at = slice(part * rows, (part + 1) * rows)
                rows_scr[block * per_block + part, kind, 0] = real[at]
                rows_scr[block * per_block + part, kind, 1] = imag[at]
    own_ref[...] = rows_scr[wide]
    for index, ref in enumerate(send_refs):
        ref[...] = rows_scr[wide ^ (index + 1)].astype(SHORT)


def expand(here, keep, came, wide_count):
    kinds, pieces, size, _ = keep.shape
    rows = pieces * size // wide_count
    shape = (kinds, 2, rows, size)
    out_shape = [jax.ShapeDtypeStruct(shape, FLOAT)]
    out_shape += [jax.ShapeDtypeStruct(shape, SHORT)] * (wide_count - 1)
    return call(
        expand_kernel,
        out_shape,
        [SMEM_SPEC, VMEM_SPEC, VMEM_SPEC],
        [pltpu.VMEM(keep.shape, FLOAT), pltpu.VMEM((wide_count,) + shape, FLOAT)],
    )(here, keep, came)


def finish_kernel(here_ref, list_ref, rows_ref, peram_ref, elem_ref, prod_ref, left_scr, right_scr):
    narrow, wide = here_ref[0], here_ref[1]
    pieces, _, _, rows, size = rows_ref.shape
    slots = list_ref.shape[0]
    wide_count, _, share, cols = peram_ref.shape
    total = pieces * size
    mine = wide * rows // size
    for slot in range(slots):
        kind = list_ref[slot]
        for block in range(pieces):
            piece = rows_ref[narrow ^ block ^ mine, kind]
            at = slice(block * size, (block + 1) * size)
            elem_ref[slot, :, :, at] = piece.astype(FLOAT)
            for r in range(2):
                left_scr[
                    slot * rows : (slot + 1) * rows,
                    r * total + block * size : r * total + (block + 1) * size,
                ] = piece[r]
    for owner in range(wide_count):
        real = peram_ref[wide ^ owner, 0]
        imag = peram_ref[wide ^ owner, 1]
        up = slice(owner * share, (owner + 1) * share)
        down = slice(total + owner * share, total + (owner + 1) * share)
        right_scr[0, up, :] = real
        right_scr[0, down, :] = -imag
        right_scr[1, up, :] = imag
        right_scr[1, down, :] = real
    for r in range(2):
        product = jnp.dot(left_scr[...], right_scr[r], preferred_element_type=FLOAT)
        for slot in range(slots):
            prod_ref[slot, r] = product[slot * rows : (slot + 1) * rows]


def finish(here, directions, rows, peram):
    pieces, _, _, row_count, size = rows.shape
    slots = directions.shape[0]
    cols = peram.shape[-1]
    total = pieces * size
    return call(
        finish_kernel,
        [
            jax.ShapeDtypeStruct((slots, 2, row_count, total), FLOAT),
            jax.ShapeDtypeStruct((slots, 2, row_count, cols), FLOAT),
        ],
        [SMEM_SPEC, SMEM_SPEC, VMEM_SPEC, VMEM_SPEC],
        [
            pltpu.VMEM((slots * row_count, 2 * total), SHORT),
            pltpu.VMEM((2, 2 * total, cols), SHORT),
        ],
    )(here, directions, rows, peram)


def gather(x, axis, masks):
    stack = x[None]
    for mask in masks:
        stack = jnp.concatenate([stack, swap(stack, axis, mask)], 0)
    return stack


def on_device(vectors, links, directions, peram):
    planes = vectors.shape[3]
    length = vectors.shape[4]
    wide_count = lax.axis_size("wide")
    narrow_count = lax.axis_size("narrow")
    norm = 1.0 / math.sqrt(12.0 * planes * wide_count * length * narrow_count)
    here = jnp.stack([lax.axis_index("narrow"), lax.axis_index("wide")]).astype(jnp.int32)
    link_rows = links.reshape(-1, length)

    vec, first, edge = split_vectors(vectors)
    plane_halo = from_behind(first, "wide", -1)
    edge_halo = from_behind(edge, "narrow", -1)
    every = tuple(range(planes))
    part = functools.partial(
        direction_part, norm=norm, pieces=narrow_count, here=here, links=link_rows, vec=vec
    )
    third = part(2, every)
    second = part(1, every, halo=edge_halo)
    inner = part(0, every[:-1], more="first")
    whole = part(0, every[-1:], halo=plane_halo, more=inner)

    parts = [whole, second, third]
    keep = jnp.stack([k for k, _ in parts])
    send = jnp.stack([s for _, s in parts])
    came = swap(send, "narrow", 1)
    for stage in range(1, narrow_count.bit_length() - 1):
        total = keep + came.astype(FLOAT)
        keep = total[:, 0::2]
        came = swap(total[:, 1::2].astype(SHORT), "narrow", 1 << stage)
    own, *sends = expand(here, keep[:, 0], came[:, 0], wide_count)
    for index, piece in enumerate(sends):
        own = own + swap(piece, "wide", index + 1).astype(FLOAT)
    masks = [1 << stage for stage in range(narrow_count.bit_length() - 1)]
    low = own.astype(SHORT)
    stack = low[None]
    for mask in reversed(masks):
        stack = jnp.concatenate([stack, swap(stack, "narrow", mask)], 0)
    order = [0]
    for mask in reversed(masks):
        order = order + [o ^ mask for o in order]
    rows = jnp.stack([stack[order.index(j)] for j in range(narrow_count)])
    peram_all = gather(peram, "wide", [1 << s for s in range(wide_count.bit_length() - 1)])
    return tuple(finish(here, directions, rows, peram_all))


def solution(mesh):
    placed = (
        P("grp", None, None, "wide", "narrow"),
        P("grp", None, None, None, "wide", "narrow"),
        P(),
        P("grp", "wide", "narrow"),
    )
    return jax.shard_map(
        on_device,
        mesh=mesh,
        in_specs=placed,
        out_specs=(P("grp", None, "wide", None), P("grp", None, "wide", "narrow")),
        check_vma=False,
    )
```

```python
import functools
import math

import jax
import jax.numpy as jnp
from jax import lax
from jax.experimental import pallas as pl
from jax.experimental.pallas import tpu as pltpu
from jax.sharding import PartitionSpec as P

LZ = 16
COMP = 6
VMEM_BYTES = 16 * 1024 * 1024
FLOAT = jnp.float32
SHORT = jnp.bfloat16

VMEM_SPEC = pl.BlockSpec(memory_space=pltpu.VMEM)
SMEM_SPEC = pl.BlockSpec(memory_space=pltpu.SMEM)


def call(kernel, out_shape, in_specs, scratch=(), flops=0, size=0):
    return pl.pallas_call(
        kernel,
        out_shape=out_shape,
        in_specs=in_specs,
        out_specs=jax.tree.map(lambda _: VMEM_SPEC, out_shape),
        scratch_shapes=list(scratch),
        compiler_params=pltpu.CompilerParams(vmem_limit_bytes=VMEM_BYTES),
        cost_estimate=pl.CostEstimate(flops=flops, bytes_accessed=size, transcendentals=0),
    )


def from_behind(x, axis, by):
    length = lax.axis_size(axis)
    return lax.ppermute(x, axis, [(i, (i + by) % length) for i in range(length)])


def swap(x, axis, mask):
    length = lax.axis_size(axis)
    return lax.ppermute(x, axis, [(i, i ^ mask) for i in range(length)])


def split_kernel(planes, x_ref, all_ref, first_ref, edge_ref, held, wide_scr, sems):
    blocks = sems.shape[0]
    count = all_ref.shape[0] // blocks
    rows = count * COMP * planes
    length = x_ref.shape[1]
    per_tile = length // LZ
    lane = lax.broadcasted_iota(jnp.int32, (count, length), 1)
    copies = []
    for block in range(blocks):
        at = pl.ds(block * rows, rows)
        copies.append(pltpu.make_async_copy(x_ref.at[at], held.at[at], sems.at[block]))
        copies[-1].start()
    for block in range(blocks):
        copies[block].wait()
        here = slice(block * count, (block + 1) * count)
        wide_scr[...] = held[block * rows : (block + 1) * rows].astype(FLOAT)
        tiles = [jnp.zeros((count, length), FLOAT)] * (edge_ref.shape[1] // length)
        for plane in range(planes):
            for comp in range(COMP):
                values = wide_scr[pl.ds(comp * planes + plane, count, stride=COMP * planes), :]
                low = values.astype(SHORT)
                at = (plane * COMP + comp) * length
                all_ref[here, at : at + length] = low
                if plane == 0:
                    first_ref[here, comp * length : (comp + 1) * length] = low
                tile, slot = divmod(plane * COMP + comp, per_tile)
                moved = values if slot == 0 else pltpu.roll(values, slot * LZ, 1)
                tiles[tile] = jnp.where(lane // LZ == slot, moved, tiles[tile])
        for tile, values in enumerate(tiles):
            edge_ref[here, tile * length : (tile + 1) * length] = values.astype(SHORT)


def split_vectors(vectors):
    count, _, _, planes, length = vectors.shape
    rows = COMP * planes
    edge_tiles = -(-rows // (length // LZ))
    blocks = 8
    shapes = [rows * length, COMP * length, edge_tiles * length]
    return call(
        functools.partial(split_kernel, planes),
        [jax.ShapeDtypeStruct((count, s), SHORT) for s in shapes],
        [pl.BlockSpec(memory_space=pltpu.HBM)],
        [
            pltpu.VMEM((count * rows, length), SHORT),
            pltpu.VMEM((count // blocks * rows, length), FLOAT),
            pltpu.SemaphoreType.DMA((blocks,)),
        ],
    )(vectors.reshape(count * rows, length))


def times_transposed(left, right):
    return lax.dot_general(left, right, (((1,), (1,)), ((), ())), preferred_element_type=FLOAT)


def direction_kernel(direction, chosen, planes, norm, has_more, has_halo, *refs):
    here_ref, links_ref, vec_ref = refs[:3]
    rest = list(refs[3:])
    halo_ref = rest.pop(0) if has_halo else None
    more_ref = rest.pop(0) if has_more is True else None
    if has_more == "first":
        whole_ref, fwd_scr, rot_scr = rest
        packed = whole_ref
    else:
        keep_ref, send_ref, fwd_scr, rot_scr, packed = rest
    count = vec_ref.shape[0]
    length = links_ref.shape[1]
    part = 3 * length
    per_tile = length // LZ
    group = 16
    lane = lax.broadcasted_iota(jnp.int32, (group, length), 1)

    def ahead(rows, plane, comp):
        at = (plane * COMP + comp) * length
        if direction == 0:
            if plane + 1 < planes:
                return vec_ref[rows, at + COMP * length : at + (COMP + 1) * length].astype(FLOAT)
            return halo_ref[rows, comp * length : (comp + 1) * length].astype(FLOAT)
        values = vec_ref[rows, at : at + length].astype(FLOAT)
        if direction == 1:
            tile, slot = divmod(plane * COMP + comp, per_tile)
            edge = halo_ref[rows, tile * length : (tile + 1) * length].astype(FLOAT)
            shift = length - LZ - slot * LZ
            edge = edge if shift == 0 else pltpu.roll(edge, shift, 1)
            return jnp.where(lane < length - LZ, pltpu.roll(values, length - LZ, 1), edge)
        return jnp.where(
            lane % LZ == LZ - 1, pltpu.roll(values, LZ - 1, 1), pltpu.roll(values, length - 1, 1)
        )

    for position, plane in enumerate(chosen):
        base = position * COMP * length

        def link(r, a, b):
            row = (((direction * 2 + r) * 3 + a) * 3 + b) * planes + plane
            return links_ref[row : row + 1, :]

        matrix = [[[link(r, a, b) for b in range(3)] for a in range(3)] for r in range(2)]

        def step(index, carry):
            rows = pl.ds(pl.multiple_of(index * group, group), group)
            real = [ahead(rows, plane, b) for b in range(3)]
            imag = [ahead(rows, plane, 3 + b) for b in range(3)]
            for a in range(3):
                out_real = sum(
                    matrix[0][a][b] * real[b] - matrix[1][a][b] * imag[b] for b in range(3)
                )
                out_imag = sum(
                    matrix[0][a][b] * imag[b] + matrix[1][a][b] * real[b] for b in range(3)
                )
                low_real = out_real.astype(SHORT)
                low_imag = out_imag.astype(SHORT)
                at = base + a * length
                fwd_scr[rows, at : at + length] = low_real
                fwd_scr[rows, at + part : at + part + length] = low_imag
                rot_scr[rows, at : at + length] = low_imag
                rot_scr[rows, at + part : at + part + length] = -low_real
            return carry

        lax.fori_loop(0, count // group, step, 0, unroll=8)

    here = here_ref[0]
    pieces = packed.shape[0]
    size = packed.shape[2]
    tile = min(256, count)
    first = chosen[0] * COMP * length
    depth = len(chosen) * COMP * length
    row = lax.broadcasted_iota(jnp.int32, (tile, tile), 0)
    col = lax.broadcasted_iota(jnp.int32, (tile, tile), 1)

    def vec(i):
        return vec_ref[i * tile : (i + 1) * tile, first : first + depth]

    def fwd(i):
        return fwd_scr[i * tile : (i + 1) * tile, :]

    def rot(i):
        return rot_scr[i * tile : (i + 1) * tile, :]

    for i in range(count // tile):
        for j in range(count // tile):
            if i < j:
                value = times_transposed(vec(i), fwd(j)) - times_transposed(fwd(i), vec(j))
            elif i > j:
                value = times_transposed(vec(i), rot(j)) + times_transposed(rot(i), vec(j))
            else:
                real = times_transposed(vec(i), fwd(i))
                imag = times_transposed(vec(i), rot(i))
                other = jnp.where(row > col, -real, imag)
                value = jnp.where(row < col, real, imag) + other.T
            value = value * norm
            for p in range(tile // size):
                for q in range(tile // size):
                    block_row = i * (tile // size) + p
                    block_col = j * (tile // size) + q
                    slot = here ^ (block_row ^ block_col)
                    block = value[p * size : (p + 1) * size, q * size : (q + 1) * size]
                    if more_ref is not None:
                        block = block + more_ref[slot, block_row]
                    packed[slot, block_row] = block
    if has_more != "first":
        for piece in range(pieces // 2):
            keep_ref[piece] = packed[2 * piece]
            send_ref[piece] = packed[2 * piece + 1].astype(SHORT)


def direction_part(direction, chosen, norm, pieces, here, links, vec, halo=None, more=None):
    planes = vec.shape[1] // (COMP * links.shape[1])
    count = vec.shape[0]
    size = count // pieces
    depth = len(chosen) * COMP * links.shape[1]
    whole = jax.ShapeDtypeStruct((pieces, pieces, size, size), FLOAT)
    if more == "first":
        out_shape = whole
    else:
        half = (pieces // 2, pieces, size, size)
        out_shape = [jax.ShapeDtypeStruct(half, FLOAT), jax.ShapeDtypeStruct(half, SHORT)]
    scratch = [pltpu.VMEM((count, depth), SHORT)] * 2
    if more != "first":
        scratch.append(pltpu.VMEM(whole.shape, FLOAT))
    operands = [here, links, vec]
    if halo is not None:
        operands.append(halo)
    has_more = more if more == "first" else more is not None
    if has_more is True:
        operands.append(more)
    return call(
        functools.partial(
            direction_kernel, direction, chosen, planes, norm, has_more, halo is not None
        ),
        out_shape,
        [SMEM_SPEC] + [VMEM_SPEC] * (len(operands) - 1),
        scratch,
        flops=1,
        size=1,
    )(*operands)


def halve_kernel(sources, *refs):
    keep_ref, send_ref = refs[-2:]
    kind = 0
    for source in range(sources):
        held, came = refs[2 * source], refs[2 * source + 1]
        for k in range(held.shape[0]):
            for piece in range(held.shape[1] // 2):
                even, odd = 2 * piece, 2 * piece + 1
                keep_ref[kind, piece] = held[k, even] + came[k, even].astype(FLOAT)
                send_ref[kind, piece] = (held[k, odd] + came[k, odd].astype(FLOAT)).astype(SHORT)
            kind += 1


def halve(*pairs):
    shape = pairs[0][0].shape
    shape = (sum(held.shape[0] for held, _ in pairs), shape[1] // 2) + shape[2:]
    return call(
        functools.partial(halve_kernel, len(pairs)),
        [jax.ShapeDtypeStruct(shape, FLOAT), jax.ShapeDtypeStruct(shape, SHORT)],
        [VMEM_SPEC] * (2 * len(pairs)),
    )(*[x for pair in pairs for x in pair])


def expand_kernel(has_extra, here_ref, keep_ref, came_ref, *refs):
    refs = list(refs)
    extra_ref = refs.pop(0) if has_extra else None
    own_ref, send_ref, sum_scr, rows_scr = refs
    narrow, wide = here_ref[0], here_ref[1]
    kinds, _, pieces, size, _ = keep_ref.shape
    half, height, _ = own_ref.shape
    rows = height // (2 * kinds)
    per_block = size // rows
    row = lax.broadcasted_iota(jnp.int32, (size, size), 0)
    col = lax.broadcasted_iota(jnp.int32, (size, size), 1)
    for kind in range(kinds):
        sum_scr[...] = keep_ref[kind, 0] + came_ref[kind, 0].astype(FLOAT)
        for block in range(pieces):
            across = narrow ^ block
            mine = sum_scr[block]
            other = sum_scr[across].T
            ahead = row + block * size - col - across * size
            real = jnp.where(ahead < 0, mine, jnp.where(ahead > 0, -other, 0.0))
            imag = jnp.where(ahead < 0, other, mine)
            for part in range(per_block):
                at = slice(part * rows, (part + 1) * rows)
                first = 2 * kind * rows
                rows_scr[block * per_block + part, first : first + rows] = real[at]
                rows_scr[block * per_block + part, first + rows : first + 2 * rows] = imag[at]
    for index in range(half):
        own_ref[index] = rows_scr[wide ^ (2 * index)]
        send_ref[index * height : (index + 1) * height] = rows_scr[wide ^ (2 * index + 1)].astype(
            SHORT
        )
    if has_extra:
        send_ref[half * height :] = extra_ref[...]


def expand(here, keep, came, wide_count, extra=None):
    kinds, _, pieces, size, _ = keep.shape
    height = kinds * 2 * pieces * size // wide_count
    half = wide_count // 2
    more = 0 if extra is None else extra.shape[0]
    operands = [here, keep, came] + ([] if extra is None else [extra])
    return call(
        functools.partial(expand_kernel, extra is not None),
        [
            jax.ShapeDtypeStruct((half, height, size), FLOAT),
            jax.ShapeDtypeStruct((half * height + more, size), SHORT),
        ],
        [SMEM_SPEC] + [VMEM_SPEC] * (len(operands) - 1),
        [
            pltpu.VMEM((pieces, size, size), FLOAT),
            pltpu.VMEM((wide_count, height, size), FLOAT),
        ],
    )(*operands)


def spread_kernel(has_extra, own_ref, came_ref, *refs):
    refs = list(refs)
    extra_ref = refs.pop(0) if has_extra else None
    keep_ref, sends = refs[0], refs[1:]
    half, height, _ = own_ref.shape
    keep_ref[...] = own_ref[0] + came_ref[:height].astype(FLOAT)
    for index in range(1, half):
        came = came_ref[index * height : (index + 1) * height].astype(FLOAT)
        sends[index - 1][:height] = (own_ref[index] + came).astype(SHORT)
        if has_extra:
            more = extra_ref.shape[0]
            sends[index - 1][height : height + more] = extra_ref[...]
            sends[index - 1][height + more :] = came_ref[half * height :]


def spread(own, came, extra=None):
    half, height, size = own.shape
    more = 0 if extra is None else 2 * extra.shape[0]
    operands = [own, came] + ([] if extra is None else [extra])
    return call(
        functools.partial(spread_kernel, extra is not None),
        [jax.ShapeDtypeStruct((height, size), FLOAT)]
        + [jax.ShapeDtypeStruct((height + more, size), SHORT)] * (half - 1),
        [VMEM_SPEC] * len(operands),
    )(*operands)


def total_kernel(sources, *refs):
    own_ref, came, rest = refs[0], refs[1 : 1 + sources], refs[1 + sources :]
    out_ref = rest[-1]
    height = own_ref.shape[0]
    total = own_ref[...]
    for ref in came:
        total = total + ref[:height].astype(FLOAT)
    out_ref[:height] = total.astype(SHORT)
    if len(rest) > 1:
        out_ref[height:] = rest[0][...]


def total(own, came, behind=None):
    height, size = own.shape
    more = 0 if behind is None else behind.shape[0]
    operands = [own, *came] + ([] if behind is None else [behind])
    return call(
        functools.partial(total_kernel, len(came)),
        jax.ShapeDtypeStruct((height + more, size), SHORT),
        [VMEM_SPEC] * len(operands),
    )(*operands)


def finish_kernel(order, here_ref, list_ref, *refs):
    pieces = len(order)
    row_refs = refs[:pieces]
    pair_ref, last_refs = refs[pieces], refs[pieces + 1 : -5]
    elem_ref, prod_ref, rows_scr, left_scr, right_scr = refs[-5:]
    narrow, wide = here_ref[0], here_ref[1]
    slots, _, rows, total = elem_ref.shape
    size = row_refs[0].shape[1]
    share = pair_ref.shape[0] // 2
    cols = pair_ref.shape[1] // 2
    height = row_refs[0].shape[0]
    mine = wide * rows // size
    for position, ref in zip(order, row_refs):
        rows_scr[position] = ref[...].reshape(slots, 2 * rows, size)
    for slot in range(slots):
        kind = list_ref[slot]
        for block in range(pieces):
            piece = rows_scr[narrow ^ block ^ mine, kind]
            at = slice(block * size, (block + 1) * size)
            for r in range(2):
                part = piece[r * rows : (r + 1) * rows]
                elem_ref[slot, r, :, at] = part.astype(FLOAT)
                left_scr[
                    slot * rows : (slot + 1) * rows,
                    r * total + block * size : r * total + (block + 1) * size,
                ] = part
    held = [pair_ref[...]]
    held += [ref[ref.shape[0] - 2 * share :, :] for ref in last_refs]
    for index, values in enumerate(held):
        for low in range(2):
            block = values[low * share : (low + 1) * share]
            turned = jnp.concatenate([-block[:, cols:], block[:, :cols]], 1)
            owner = wide ^ (2 * index + low)
            right_scr[0, owner] = block
            right_scr[1, owner] = turned
    right = right_scr[...].reshape(2 * total, 2 * cols)
    product = jnp.dot(left_scr[...], right, preferred_element_type=FLOAT)
    for slot in range(slots):
        for r in range(2):
            prod_ref[slot, r] = product[
                slot * rows : (slot + 1) * rows, r * cols : (r + 1) * cols
            ]


def finish(here, directions, order, rows, pair, last):
    pieces = len(rows)
    slots = directions.shape[0]
    height, size = rows[0].shape
    row_count = height // (2 * slots)
    share, cols = pair.shape[0] // 2, pair.shape[1] // 2
    total = pieces * size
    operands = [*rows, pair, *last]
    return call(
        functools.partial(finish_kernel, order),
        [
            jax.ShapeDtypeStruct((slots, 2, row_count, total), FLOAT),
            jax.ShapeDtypeStruct((slots, 2, row_count, cols), FLOAT),
        ],
        [SMEM_SPEC, SMEM_SPEC] + [VMEM_SPEC] * len(operands),
        [
            pltpu.VMEM((pieces, slots, 2 * row_count, size), SHORT),
            pltpu.VMEM((slots * row_count, 2 * total), SHORT),
            pltpu.VMEM((2, total // share, share, 2 * cols), SHORT),
        ],
    )(here, directions, *operands)


def on_device(vectors, links, directions, peram):
    planes = vectors.shape[3]
    length = vectors.shape[4]
    wide_count = lax.axis_size("wide")
    narrow_count = lax.axis_size("narrow")
    norm = 1.0 / math.sqrt(12.0 * planes * wide_count * length * narrow_count)
    here = jnp.stack([lax.axis_index("narrow"), lax.axis_index("wide")]).astype(jnp.int32)
    link_rows = links.reshape(-1, length)
    pair = jnp.concatenate([peram[0], peram[1]], 1)

    vec, first, edge = split_vectors(vectors)
    plane_halo = from_behind(first, "wide", -1)
    edge_halo = from_behind(edge, "narrow", -1)
    every = tuple(range(planes))
    part = functools.partial(
        direction_part, norm=norm, pieces=narrow_count, here=here, links=link_rows, vec=vec
    )

    def over_narrow(parts, tie=None):
        keep, send = halve(*[(k[None], swap(s, "narrow", 1)[None]) for k, s in parts])
        if tie is not None:
            keep, send, tie = lax.optimization_barrier((keep, send, tie))
        for stage in range(1, narrow_count.bit_length() - 1):
            came = swap(send, "narrow", 1 << stage)
            if keep.shape[1] > 1:
                keep, send = halve((keep, came))
        return keep, came, tie

    def over_wide(own, send, extra=None):
        came = swap(send, "wide", 1)
        own, *sends = spread(own, came, extra)
        return own, came, [swap(x, "wide", 2 * (i + 1)) for i, x in enumerate(sends)]

    third = part(2, every)
    second = part(1, every, halo=edge_halo)
    inner = part(0, every[:-1], more="first")
    keep, came, plane_halo = over_narrow([second, third], plane_halo)
    own, near, far = over_wide(*expand(here, keep, came, wide_count, pair), pair)
    early = total(own, far)
    pairs = jnp.concatenate([pair, near[near.shape[0] - pair.shape[0] :]], 0)

    whole = part(0, every[-1:], halo=plane_halo, more=inner)
    keep, came, _ = over_narrow([whole])
    own, _, late = over_wide(*expand(here, keep, came, wide_count))
    rows = [total(own, late, early)]
    order = [0]
    for stage in reversed(range(narrow_count.bit_length() - 1)):
        rows = rows + [swap(x, "narrow", 1 << stage) for x in rows]
        order = order + [o ^ (1 << stage) for o in order]
    return tuple(finish(here, directions, order, rows, pairs, far))


def solution(mesh):
    placed = (
        P("grp", None, None, "wide", "narrow"),
        P("grp", None, None, None, "wide", "narrow"),
        P(),
        P("grp", "wide", "narrow"),
    )
    return jax.shard_map(
        on_device,
        mesh=mesh,
        in_specs=placed,
        out_specs=(P("grp", None, "wide", None), P("grp", None, "wide", "narrow")),
        check_vma=False,
    )
```

```python
import functools
import math

import jax
import jax.numpy as jnp
from jax import lax
from jax.experimental import pallas as pl
from jax.experimental.pallas import tpu as pltpu
from jax.sharding import PartitionSpec as P

LZ = 16
COMP = 6
VMEM_BYTES = 16 * 1024 * 1024
FLOAT = jnp.float32
SHORT = jnp.bfloat16

VMEM_SPEC = pl.BlockSpec(memory_space=pltpu.VMEM)
SMEM_SPEC = pl.BlockSpec(memory_space=pltpu.SMEM)


def call(kernel, out_shape, in_specs, scratch=()):
    return pl.pallas_call(
        kernel,
        out_shape=out_shape,
        in_specs=in_specs,
        out_specs=jax.tree.map(lambda _: VMEM_SPEC, out_shape),
        scratch_shapes=list(scratch),
        compiler_params=pltpu.CompilerParams(vmem_limit_bytes=VMEM_BYTES),
        cost_estimate=pl.CostEstimate(flops=1, bytes_accessed=1, transcendentals=0),
    )


def from_behind(x, axis, by):
    length = lax.axis_size(axis)
    return lax.ppermute(x, axis, [(i, (i + by) % length) for i in range(length)])


def swap(x, axis, mask):
    length = lax.axis_size(axis)
    return lax.ppermute(x, axis, [(i, i ^ mask) for i in range(length)])


def front_kernel(planes, x_ref, first_ref, wide_scr):
    count = first_ref.shape[0]
    length = x_ref.shape[1]
    wide_scr[...] = x_ref[...].astype(FLOAT)
    for comp in range(COMP):
        values = wide_scr[pl.ds(comp * planes, count, stride=COMP * planes), :]
        first_ref[:, comp * length : (comp + 1) * length] = values.astype(SHORT)


def split_kernel(planes, x_ref, all_ref, edge_ref, wide_scr):
    count = all_ref.shape[0]
    length = x_ref.shape[1]
    per_tile = length // LZ
    wide_scr[...] = x_ref[...].astype(FLOAT)
    lane = lax.broadcasted_iota(jnp.int32, (count, length), 1)
    tiles = [jnp.zeros((count, length), FLOAT)] * (edge_ref.shape[1] // length)
    for plane in range(planes):
        for comp in range(COMP):
            values = wide_scr[pl.ds(comp * planes + plane, count, stride=COMP * planes), :]
            at = (plane * COMP + comp) * length
            all_ref[:, at : at + length] = values.astype(SHORT)
            tile, slot = divmod(plane * COMP + comp, per_tile)
            moved = values if slot == 0 else pltpu.roll(values, slot * LZ, 1)
            tiles[tile] = jnp.where(lane // LZ == slot, moved, tiles[tile])
    for tile, values in enumerate(tiles):
        edge_ref[:, tile * length : (tile + 1) * length] = values.astype(SHORT)


def by_rows(kernel, flat, count, planes, widths, block):
    rows = COMP * planes
    length = flat.shape[1]
    return pl.pallas_call(
        functools.partial(kernel, planes),
        grid=(count // block,),
        out_shape=[jax.ShapeDtypeStruct((count, width), SHORT) for width in widths],
        in_specs=[pl.BlockSpec((block * rows, length), lambda i: (i, 0))],
        out_specs=[pl.BlockSpec((block, width), lambda i: (i, 0)) for width in widths],
        scratch_shapes=[pltpu.VMEM((block * rows, length), FLOAT)],
        compiler_params=pltpu.CompilerParams(vmem_limit_bytes=VMEM_BYTES),
        cost_estimate=pl.CostEstimate(flops=1, bytes_accessed=1, transcendentals=0),
    )(flat)


def split_vectors(vectors):
    count, _, _, planes, length = vectors.shape
    flat = vectors.reshape(-1, length)
    edge_tiles = -(-COMP * planes // (length // LZ))
    (first,) = by_rows(front_kernel, flat, count, planes, [COMP * length], 64)
    _, flat = lax.optimization_barrier((first, flat))
    widths = [COMP * planes * length, edge_tiles * length]
    vec, edge = by_rows(split_kernel, flat, count, planes, widths, 256)
    return vec, first, edge


def times_transposed(left, right):
    return lax.dot_general(left, right, (((1,), (1,)), ((), ())), preferred_element_type=FLOAT)


def direction_kernel(direction, chosen, planes, norm, has_more, has_halo, *refs):
    here_ref, links_ref, vec_ref = refs[:3]
    rest = list(refs[3:])
    halo_ref = rest.pop(0) if has_halo else None
    more_ref = rest.pop(0) if has_more is True else None
    if has_more == "first":
        whole_ref, fwd_scr, rot_scr = rest
        packed = whole_ref
    else:
        keep_ref, send_ref, fwd_scr, rot_scr, packed = rest
    count = vec_ref.shape[0]
    length = links_ref.shape[1]
    part = 3 * length
    per_tile = length // LZ
    group = 16
    lane = lax.broadcasted_iota(jnp.int32, (group, length), 1)

    def ahead(rows, plane, comp):
        at = (plane * COMP + comp) * length
        if direction == 0:
            if plane + 1 < planes:
                return vec_ref[rows, at + COMP * length : at + (COMP + 1) * length].astype(FLOAT)
            return halo_ref[rows, comp * length : (comp + 1) * length].astype(FLOAT)
        values = vec_ref[rows, at : at + length].astype(FLOAT)
        if direction == 1:
            tile, slot = divmod(plane * COMP + comp, per_tile)
            edge = halo_ref[rows, tile * length : (tile + 1) * length].astype(FLOAT)
            shift = length - LZ - slot * LZ
            edge = edge if shift == 0 else pltpu.roll(edge, shift, 1)
            return jnp.where(lane < length - LZ, pltpu.roll(values, length - LZ, 1), edge)
        return jnp.where(
            lane % LZ == LZ - 1, pltpu.roll(values, LZ - 1, 1), pltpu.roll(values, length - 1, 1)
        )

    for position, plane in enumerate(chosen):
        base = position * COMP * length

        def link(r, a, b):
            row = (((direction * 2 + r) * 3 + a) * 3 + b) * planes + plane
            return links_ref[row : row + 1, :]

        matrix = [[[link(r, a, b) for b in range(3)] for a in range(3)] for r in range(2)]

        def step(index, carry):
            rows = pl.ds(pl.multiple_of(index * group, group), group)
            real = [ahead(rows, plane, b) for b in range(3)]
            imag = [ahead(rows, plane, 3 + b) for b in range(3)]
            for a in range(3):
                out_real = sum(
                    matrix[0][a][b] * real[b] - matrix[1][a][b] * imag[b] for b in range(3)
                )
                out_imag = sum(
                    matrix[0][a][b] * imag[b] + matrix[1][a][b] * real[b] for b in range(3)
                )
                low_real = out_real.astype(SHORT)
                low_imag = out_imag.astype(SHORT)
                at = base + a * length
                fwd_scr[rows, at : at + length] = low_real
                fwd_scr[rows, at + part : at + part + length] = low_imag
                rot_scr[rows, at : at + length] = low_imag
                rot_scr[rows, at + part : at + part + length] = -low_real
            return carry

        lax.fori_loop(0, count // group, step, 0, unroll=8)

    here = here_ref[0]
    pieces = packed.shape[0]
    size = packed.shape[2]
    tile = min(256, count)
    first = chosen[0] * COMP * length
    depth = len(chosen) * COMP * length
    row = lax.broadcasted_iota(jnp.int32, (tile, tile), 0)
    col = lax.broadcasted_iota(jnp.int32, (tile, tile), 1)

    def vec(i):
        return vec_ref[i * tile : (i + 1) * tile, first : first + depth]

    def fwd(i):
        return fwd_scr[i * tile : (i + 1) * tile, :]

    def rot(i):
        return rot_scr[i * tile : (i + 1) * tile, :]

    for i in range(count // tile):
        for j in range(count // tile):
            if i < j:
                value = times_transposed(vec(i), fwd(j)) - times_transposed(fwd(i), vec(j))
            elif i > j:
                value = times_transposed(vec(i), rot(j)) + times_transposed(rot(i), vec(j))
            else:
                real = times_transposed(vec(i), fwd(i))
                imag = times_transposed(vec(i), rot(i))
                other = jnp.where(row > col, -real, imag)
                value = jnp.where(row < col, real, imag) + other.T
            value = value * norm
            for p in range(tile // size):
                for q in range(tile // size):
                    block_row = i * (tile // size) + p
                    block_col = j * (tile // size) + q
                    slot = here ^ (block_row ^ block_col)
                    block = value[p * size : (p + 1) * size, q * size : (q + 1) * size]
                    if more_ref is not None:
                        block = block + more_ref[slot, block_row]
                    packed[slot, block_row] = block
    if has_more != "first":
        for piece in range(pieces // 2):
            keep_ref[piece] = packed[2 * piece]
            send_ref[piece] = packed[2 * piece + 1].astype(SHORT)


def direction_part(direction, chosen, norm, pieces, here, links, vec, halo=None, more=None):
    planes = vec.shape[1] // (COMP * links.shape[1])
    count = vec.shape[0]
    size = count // pieces
    depth = len(chosen) * COMP * links.shape[1]
    whole = jax.ShapeDtypeStruct((pieces, pieces, size, size), FLOAT)
    if more == "first":
        out_shape = whole
    else:
        half = (pieces // 2, pieces, size, size)
        out_shape = [jax.ShapeDtypeStruct(half, FLOAT), jax.ShapeDtypeStruct(half, SHORT)]
    scratch = [pltpu.VMEM((count, depth), SHORT)] * 2
    if more != "first":
        scratch.append(pltpu.VMEM(whole.shape, FLOAT))
    operands = [here, links, vec]
    if halo is not None:
        operands.append(halo)
    has_more = more if more == "first" else more is not None
    if has_more is True:
        operands.append(more)
    return call(
        functools.partial(
            direction_kernel, direction, chosen, planes, norm, has_more, halo is not None
        ),
        out_shape,
        [SMEM_SPEC] + [VMEM_SPEC] * (len(operands) - 1),
        scratch,
    )(*operands)


def halve_kernel(sources, *refs):
    keep_ref, send_ref = refs[-2:]
    kind = 0
    for source in range(sources):
        held, came = refs[2 * source], refs[2 * source + 1]
        for k in range(held.shape[0]):
            for piece in range(held.shape[1] // 2):
                even, odd = 2 * piece, 2 * piece + 1
                keep_ref[kind, piece] = held[k, even] + came[k, even].astype(FLOAT)
                send_ref[kind, piece] = (held[k, odd] + came[k, odd].astype(FLOAT)).astype(SHORT)
            kind += 1


def halve(*pairs):
    shape = pairs[0][0].shape
    shape = (sum(held.shape[0] for held, _ in pairs), shape[1] // 2) + shape[2:]
    return call(
        functools.partial(halve_kernel, len(pairs)),
        [jax.ShapeDtypeStruct(shape, FLOAT), jax.ShapeDtypeStruct(shape, SHORT)],
        [VMEM_SPEC] * (2 * len(pairs)),
    )(*[x for pair in pairs for x in pair])


def expand_kernel(has_extra, here_ref, keep_ref, came_ref, *refs):
    refs = list(refs)
    extra_ref = refs.pop(0) if has_extra else None
    own_ref, send_ref, sum_scr, rows_scr = refs
    narrow, wide = here_ref[0], here_ref[1]
    kinds, _, pieces, size, _ = keep_ref.shape
    half, height, _ = own_ref.shape
    rows = height // (2 * kinds)
    per_block = size // rows
    row = lax.broadcasted_iota(jnp.int32, (size, size), 0)
    col = lax.broadcasted_iota(jnp.int32, (size, size), 1)
    for kind in range(kinds):
        sum_scr[...] = keep_ref[kind, 0] + came_ref[kind, 0].astype(FLOAT)
        for block in range(pieces):
            across = narrow ^ block
            mine = sum_scr[block]
            other = sum_scr[across].T
            ahead = row + block * size - col - across * size
            real = jnp.where(ahead < 0, mine, jnp.where(ahead > 0, -other, 0.0))
            imag = jnp.where(ahead < 0, other, mine)
            for part in range(per_block):
                at = slice(part * rows, (part + 1) * rows)
                first = 2 * kind * rows
                rows_scr[block * per_block + part, first : first + rows] = real[at]
                rows_scr[block * per_block + part, first + rows : first + 2 * rows] = imag[at]
    for index in range(half):
        own_ref[index] = rows_scr[wide ^ (2 * index)]
        send_ref[index * height : (index + 1) * height] = rows_scr[wide ^ (2 * index + 1)].astype(
            SHORT
        )
    if has_extra:
        send_ref[half * height :] = extra_ref[...]


def expand(here, keep, came, wide_count, extra=None):
    kinds, _, pieces, size, _ = keep.shape
    height = kinds * 2 * pieces * size // wide_count
    half = wide_count // 2
    more = 0 if extra is None else extra.shape[0]
    operands = [here, keep, came] + ([] if extra is None else [extra])
    return call(
        functools.partial(expand_kernel, extra is not None),
        [
            jax.ShapeDtypeStruct((half, height, size), FLOAT),
            jax.ShapeDtypeStruct((half * height + more, size), SHORT),
        ],
        [SMEM_SPEC] + [VMEM_SPEC] * (len(operands) - 1),
        [
            pltpu.VMEM((pieces, size, size), FLOAT),
            pltpu.VMEM((wide_count, height, size), FLOAT),
        ],
    )(*operands)


def spread_kernel(has_extra, own_ref, came_ref, *refs):
    refs = list(refs)
    extra_ref = refs.pop(0) if has_extra else None
    keep_ref, sends = refs[0], refs[1:]
    half, height, _ = own_ref.shape
    keep_ref[...] = own_ref[0] + came_ref[:height].astype(FLOAT)
    for index in range(1, half):
        came = came_ref[index * height : (index + 1) * height].astype(FLOAT)
        sends[index - 1][:height] = (own_ref[index] + came).astype(SHORT)
        if has_extra:
            more = extra_ref.shape[0]
            sends[index - 1][height : height + more] = extra_ref[...]
            sends[index - 1][height + more :] = came_ref[half * height :]


def spread(own, came, extra=None):
    half, height, size = own.shape
    more = 0 if extra is None else 2 * extra.shape[0]
    operands = [own, came] + ([] if extra is None else [extra])
    return call(
        functools.partial(spread_kernel, extra is not None),
        [jax.ShapeDtypeStruct((height, size), FLOAT)]
        + [jax.ShapeDtypeStruct((height + more, size), SHORT)] * (half - 1),
        [VMEM_SPEC] * len(operands),
    )(*operands)


def total_kernel(sources, *refs):
    own_ref, came, rest = refs[0], refs[1 : 1 + sources], refs[1 + sources :]
    out_ref = rest[-1]
    height = own_ref.shape[0]
    total = own_ref[...]
    for ref in came:
        total = total + ref[:height].astype(FLOAT)
    out_ref[:height] = total.astype(SHORT)
    if len(rest) > 1:
        out_ref[height:] = rest[0][...]


def total(own, came, behind=None):
    height, size = own.shape
    more = 0 if behind is None else behind.shape[0]
    operands = [own, *came] + ([] if behind is None else [behind])
    return call(
        functools.partial(total_kernel, len(came)),
        jax.ShapeDtypeStruct((height + more, size), SHORT),
        [VMEM_SPEC] * len(operands),
    )(*operands)


def finish_kernel(order, here_ref, list_ref, *refs):
    pieces = len(order)
    row_refs = refs[:pieces]
    pair_ref, last_refs = refs[pieces], refs[pieces + 1 : -5]
    elem_ref, prod_ref, rows_scr, left_scr, right_scr = refs[-5:]
    narrow, wide = here_ref[0], here_ref[1]
    slots, _, rows, total = elem_ref.shape
    size = row_refs[0].shape[1]
    share = pair_ref.shape[0] // 2
    cols = pair_ref.shape[1] // 2
    height = row_refs[0].shape[0]
    mine = wide * rows // size
    for position, ref in zip(order, row_refs):
        rows_scr[position] = ref[...].reshape(slots, 2 * rows, size)
    for slot in range(slots):
        kind = list_ref[slot]
        for block in range(pieces):
            piece = rows_scr[narrow ^ block ^ mine, kind]
            at = slice(block * size, (block + 1) * size)
            for r in range(2):
                part = piece[r * rows : (r + 1) * rows]
                elem_ref[slot, r, :, at] = part.astype(FLOAT)
                left_scr[
                    slot * rows : (slot + 1) * rows,
                    r * total + block * size : r * total + (block + 1) * size,
                ] = part
    held = [pair_ref[...]]
    held += [ref[ref.shape[0] - 2 * share :, :] for ref in last_refs]
    for index, values in enumerate(held):
        for low in range(2):
            block = values[low * share : (low + 1) * share]
            turned = jnp.concatenate([-block[:, cols:], block[:, :cols]], 1)
            owner = wide ^ (2 * index + low)
            right_scr[0, owner] = block
            right_scr[1, owner] = turned
    right = right_scr[...].reshape(2 * total, 2 * cols)
    product = jnp.dot(left_scr[...], right, preferred_element_type=FLOAT)
    for slot in range(slots):
        for r in range(2):
            prod_ref[slot, r] = product[
                slot * rows : (slot + 1) * rows, r * cols : (r + 1) * cols
            ]


def finish(here, directions, order, rows, pair, last):
    pieces = len(rows)
    slots = directions.shape[0]
    height, size = rows[0].shape
    row_count = height // (2 * slots)
    share, cols = pair.shape[0] // 2, pair.shape[1] // 2
    total = pieces * size
    operands = [*rows, pair, *last]
    return call(
        functools.partial(finish_kernel, order),
        [
            jax.ShapeDtypeStruct((slots, 2, row_count, total), FLOAT),
            jax.ShapeDtypeStruct((slots, 2, row_count, cols), FLOAT),
        ],
        [SMEM_SPEC, SMEM_SPEC] + [VMEM_SPEC] * len(operands),
        [
            pltpu.VMEM((pieces, slots, 2 * row_count, size), SHORT),
            pltpu.VMEM((slots * row_count, 2 * total), SHORT),
            pltpu.VMEM((2, total // share, share, 2 * cols), SHORT),
        ],
    )(here, directions, *operands)


def on_device(vectors, links, directions, peram):
    planes = vectors.shape[3]
    length = vectors.shape[4]
    wide_count = lax.axis_size("wide")
    narrow_count = lax.axis_size("narrow")
    norm = 1.0 / math.sqrt(12.0 * planes * wide_count * length * narrow_count)
    here = jnp.stack([lax.axis_index("narrow"), lax.axis_index("wide")]).astype(jnp.int32)
    link_rows = links.reshape(-1, length)
    pair = jnp.concatenate([peram[0], peram[1]], 1)

    vec, first, edge = split_vectors(vectors)
    plane_halo = from_behind(first, "wide", -1)
    edge_halo = from_behind(edge, "narrow", -1)
    every = tuple(range(planes))
    part = functools.partial(
        direction_part, norm=norm, pieces=narrow_count, here=here, links=link_rows, vec=vec
    )

    def over_narrow(parts, tie=None):
        keep, send = halve(*[(k[None], swap(s, "narrow", 1)[None]) for k, s in parts])
        if tie is not None:
            _, tie = lax.optimization_barrier((keep, tie))
        for stage in range(1, narrow_count.bit_length() - 1):
            came = swap(send, "narrow", 1 << stage)
            if keep.shape[1] > 1:
                keep, send = halve((keep, came))
        return keep, came, tie

    def over_wide(own, send, extra=None):
        came = swap(send, "wide", 1)
        own, *sends = spread(own, came, extra)
        return own, came, [swap(x, "wide", 2 * (i + 1)) for i, x in enumerate(sends)]

    third = part(2, every)
    second = part(1, every, halo=edge_halo)
    inner = part(0, every[:-1], more="first")
    keep, came, plane_halo = over_narrow([second, third], plane_halo)
    early, near, far = over_wide(*expand(here, keep, came, wide_count, pair), pair)
    whole = part(0, every[-1:], halo=plane_halo, more=inner)
    keep, came, _ = over_narrow([whole])
    _, came = lax.optimization_barrier((early, came))
    late, _, rest = over_wide(*expand(here, keep, came, wide_count))
    pairs = jnp.concatenate([pair, near[near.shape[0] - pair.shape[0] :]], 0)

    rows = [total(late, rest, total(early, far))]
    order = [0]
    for stage in reversed(range(narrow_count.bit_length() - 1)):
        rows = rows + [swap(x, "narrow", 1 << stage) for x in rows]
        order = order + [o ^ (1 << stage) for o in order]
    return tuple(finish(here, directions, order, rows, pairs, far))


def solution(mesh):
    placed = (
        P("grp", None, None, "wide", "narrow"),
        P("grp", None, None, None, "wide", "narrow"),
        P(),
        P("grp", "wide", "narrow"),
    )
    return jax.shard_map(
        on_device,
        mesh=mesh,
        in_specs=placed,
        out_specs=(P("grp", None, "wide", None), P("grp", None, "wide", "narrow")),
        check_vma=False,
    )
```

```python
import functools
import math

import jax
import jax.numpy as jnp
from jax import lax
from jax.experimental import pallas as pl
from jax.experimental.pallas import tpu as pltpu
from jax.sharding import PartitionSpec as P

LZ = 16
COMP = 6
VMEM_BYTES = 16 * 1024 * 1024
FLOAT = jnp.float32
SHORT = jnp.bfloat16

VMEM_SPEC = pl.BlockSpec(memory_space=pltpu.VMEM)
SMEM_SPEC = pl.BlockSpec(memory_space=pltpu.SMEM)


def call(kernel, out_shape, in_specs, scratch=()):
    return pl.pallas_call(
        kernel,
        out_shape=out_shape,
        in_specs=in_specs,
        out_specs=jax.tree.map(lambda _: VMEM_SPEC, out_shape),
        scratch_shapes=list(scratch),
        compiler_params=pltpu.CompilerParams(vmem_limit_bytes=VMEM_BYTES),
        cost_estimate=pl.CostEstimate(flops=1, bytes_accessed=1, transcendentals=0),
    )


def from_behind(x, axis, by):
    length = lax.axis_size(axis)
    return lax.ppermute(x, axis, [(i, (i + by) % length) for i in range(length)])


def swap(x, axis, mask):
    length = lax.axis_size(axis)
    return lax.ppermute(x, axis, [(i, i ^ mask) for i in range(length)])


def front_kernel(planes, x_ref, first_ref, wide_scr):
    count = first_ref.shape[0]
    length = x_ref.shape[1]
    wide_scr[...] = x_ref[...].astype(FLOAT)
    for comp in range(COMP):
        values = wide_scr[pl.ds(comp * planes, count, stride=COMP * planes), :]
        first_ref[:, comp * length : (comp + 1) * length] = values.astype(SHORT)


def split_kernel(planes, x_ref, all_ref, edge_ref, wide_scr):
    count = all_ref.shape[0]
    length = x_ref.shape[1]
    per_tile = length // LZ
    wide_scr[...] = x_ref[...].astype(FLOAT)
    lane = lax.broadcasted_iota(jnp.int32, (count, length), 1)
    tiles = [jnp.zeros((count, length), FLOAT)] * (edge_ref.shape[1] // length)
    for plane in range(planes):
        for comp in range(COMP):
            values = wide_scr[pl.ds(comp * planes + plane, count, stride=COMP * planes), :]
            at = (plane * COMP + comp) * length
            all_ref[:, at : at + length] = values.astype(SHORT)
            tile, slot = divmod(plane * COMP + comp, per_tile)
            moved = values if slot == 0 else pltpu.roll(values, slot * LZ, 1)
            tiles[tile] = jnp.where(lane // LZ == slot, moved, tiles[tile])
    for tile, values in enumerate(tiles):
        edge_ref[:, tile * length : (tile + 1) * length] = values.astype(SHORT)


def by_rows(kernel, flat, count, planes, widths, block):
    rows = COMP * planes
    length = flat.shape[1]
    return pl.pallas_call(
        functools.partial(kernel, planes),
        grid=(count // block,),
        out_shape=[jax.ShapeDtypeStruct((count, width), SHORT) for width in widths],
        in_specs=[pl.BlockSpec((block * rows, length), lambda i: (i, 0))],
        out_specs=[pl.BlockSpec((block, width), lambda i: (i, 0)) for width in widths],
        scratch_shapes=[pltpu.VMEM((block * rows, length), FLOAT)],
        compiler_params=pltpu.CompilerParams(vmem_limit_bytes=VMEM_BYTES),
        cost_estimate=pl.CostEstimate(flops=1, bytes_accessed=1, transcendentals=0),
    )(flat)


def split_vectors(vectors):
    count, _, _, planes, length = vectors.shape
    flat = vectors.reshape(-1, length)
    edge_tiles = -(-COMP * planes // (length // LZ))
    (first,) = by_rows(front_kernel, flat, count, planes, [COMP * length], 64)
    _, flat = lax.optimization_barrier((first, flat))
    widths = [COMP * planes * length, edge_tiles * length]
    vec, edge = by_rows(split_kernel, flat, count, planes, widths, 256)
    return vec, first, edge


def times_transposed(left, right):
    return lax.dot_general(left, right, (((1,), (1,)), ((), ())), preferred_element_type=FLOAT)


def direction_kernel(direction, chosen, planes, norm, has_more, has_halo, *refs):
    here_ref, links_ref, vec_ref = refs[:3]
    rest = list(refs[3:])
    halo_ref = rest.pop(0) if has_halo else None
    more_ref = rest.pop(0) if has_more is True else None
    if has_more == "first":
        whole_ref, fwd_scr, rot_scr = rest
        packed = whole_ref
    else:
        keep_ref, send_ref, fwd_scr, rot_scr, packed = rest
    count = vec_ref.shape[0]
    length = links_ref.shape[1]
    part = 3 * length
    per_tile = length // LZ
    group = 16
    lane = lax.broadcasted_iota(jnp.int32, (group, length), 1)

    def ahead(rows, plane, comp):
        at = (plane * COMP + comp) * length
        if direction == 0:
            if plane + 1 < planes:
                return vec_ref[rows, at + COMP * length : at + (COMP + 1) * length].astype(FLOAT)
            return halo_ref[rows, comp * length : (comp + 1) * length].astype(FLOAT)
        values = vec_ref[rows, at : at + length].astype(FLOAT)
        if direction == 1:
            tile, slot = divmod(plane * COMP + comp, per_tile)
            edge = halo_ref[rows, tile * length : (tile + 1) * length].astype(FLOAT)
            shift = length - LZ - slot * LZ
            edge = edge if shift == 0 else pltpu.roll(edge, shift, 1)
            return jnp.where(lane < length - LZ, pltpu.roll(values, length - LZ, 1), edge)
        return jnp.where(
            lane % LZ == LZ - 1, pltpu.roll(values, LZ - 1, 1), pltpu.roll(values, length - 1, 1)
        )

    for position, plane in enumerate(chosen):
        base = position * COMP * length

        def link(r, a, b):
            row = (((direction * 2 + r) * 3 + a) * 3 + b) * planes + plane
            return links_ref[row : row + 1, :]

        matrix = [[[link(r, a, b) for b in range(3)] for a in range(3)] for r in range(2)]

        def step(index, carry):
            rows = pl.ds(pl.multiple_of(index * group, group), group)
            real = [ahead(rows, plane, b) for b in range(3)]
            imag = [ahead(rows, plane, 3 + b) for b in range(3)]
            for a in range(3):
                out_real = sum(
                    matrix[0][a][b] * real[b] - matrix[1][a][b] * imag[b] for b in range(3)
                )
                out_imag = sum(
                    matrix[0][a][b] * imag[b] + matrix[1][a][b] * real[b] for b in range(3)
                )
                low_real = out_real.astype(SHORT)
                low_imag = out_imag.astype(SHORT)
                at = base + a * length
                fwd_scr[rows, at : at + length] = low_real
                fwd_scr[rows, at + part : at + part + length] = low_imag
                rot_scr[rows, at : at + length] = low_imag
                rot_scr[rows, at + part : at + part + length] = -low_real
            return carry

        lax.fori_loop(0, count // group, step, 0, unroll=8)

    here = here_ref[0]
    pieces = packed.shape[0]
    size = packed.shape[2]
    tile = min(256, count)
    first = chosen[0] * COMP * length
    depth = len(chosen) * COMP * length
    row = lax.broadcasted_iota(jnp.int32, (tile, tile), 0)
    col = lax.broadcasted_iota(jnp.int32, (tile, tile), 1)

    def vec(i):
        return vec_ref[i * tile : (i + 1) * tile, first : first + depth]

    def fwd(i):
        return fwd_scr[i * tile : (i + 1) * tile, :]

    def rot(i):
        return rot_scr[i * tile : (i + 1) * tile, :]

    for i in range(count // tile):
        for j in range(count // tile):
            if i < j:
                value = times_transposed(vec(i), fwd(j)) - times_transposed(fwd(i), vec(j))
            elif i > j:
                value = times_transposed(vec(i), rot(j)) + times_transposed(rot(i), vec(j))
            else:
                real = times_transposed(vec(i), fwd(i))
                imag = times_transposed(vec(i), rot(i))
                other = jnp.where(row > col, -real, imag)
                value = jnp.where(row < col, real, imag) + other.T
            value = value * norm
            for p in range(tile // size):
                for q in range(tile // size):
                    block_row = i * (tile // size) + p
                    block_col = j * (tile // size) + q
                    slot = here ^ (block_row ^ block_col)
                    block = value[p * size : (p + 1) * size, q * size : (q + 1) * size]
                    if more_ref is not None:
                        block = block + more_ref[slot, block_row]
                    packed[slot, block_row] = block
    if has_more != "first":
        for piece in range(pieces // 2):
            keep_ref[piece] = packed[2 * piece]
            send_ref[piece] = packed[2 * piece + 1].astype(SHORT)


def direction_part(direction, chosen, norm, pieces, here, links, vec, halo=None, more=None):
    planes = vec.shape[1] // (COMP * links.shape[1])
    count = vec.shape[0]
    size = count // pieces
    depth = len(chosen) * COMP * links.shape[1]
    whole = jax.ShapeDtypeStruct((pieces, pieces, size, size), FLOAT)
    if more == "first":
        out_shape = whole
    else:
        half = (pieces // 2, pieces, size, size)
        out_shape = [jax.ShapeDtypeStruct(half, FLOAT), jax.ShapeDtypeStruct(half, SHORT)]
    scratch = [pltpu.VMEM((count, depth), SHORT)] * 2
    if more != "first":
        scratch.append(pltpu.VMEM(whole.shape, FLOAT))
    operands = [here, links, vec]
    if halo is not None:
        operands.append(halo)
    has_more = more if more == "first" else more is not None
    if has_more is True:
        operands.append(more)
    return call(
        functools.partial(
            direction_kernel, direction, chosen, planes, norm, has_more, halo is not None
        ),
        out_shape,
        [SMEM_SPEC] + [VMEM_SPEC] * (len(operands) - 1),
        scratch,
    )(*operands)


def halve_kernel(sources, *refs):
    keep_ref, send_ref = refs[-2:]
    kind = 0
    for source in range(sources):
        held, came = refs[2 * source], refs[2 * source + 1]
        for k in range(held.shape[0]):
            for piece in range(held.shape[1] // 2):
                even, odd = 2 * piece, 2 * piece + 1
                keep_ref[kind, piece] = held[k, even] + came[k, even].astype(FLOAT)
                send_ref[kind, piece] = (held[k, odd] + came[k, odd].astype(FLOAT)).astype(SHORT)
            kind += 1


def halve(*pairs):
    shape = pairs[0][0].shape
    shape = (sum(held.shape[0] for held, _ in pairs), shape[1] // 2) + shape[2:]
    return call(
        functools.partial(halve_kernel, len(pairs)),
        [jax.ShapeDtypeStruct(shape, FLOAT), jax.ShapeDtypeStruct(shape, SHORT)],
        [VMEM_SPEC] * (2 * len(pairs)),
    )(*[x for pair in pairs for x in pair])


def expand_kernel(has_extra, here_ref, keep_ref, came_ref, *refs):
    refs = list(refs)
    extra_ref = refs.pop(0) if has_extra else None
    own_ref, send_ref, sum_scr, rows_scr = refs
    narrow, wide = here_ref[0], here_ref[1]
    kinds, _, pieces, size, _ = keep_ref.shape
    half, height, _ = own_ref.shape
    rows = height // (2 * kinds)
    per_block = size // rows
    row = lax.broadcasted_iota(jnp.int32, (size, size), 0)
    col = lax.broadcasted_iota(jnp.int32, (size, size), 1)
    for kind in range(kinds):
        sum_scr[...] = keep_ref[kind, 0] + came_ref[kind, 0].astype(FLOAT)
        for block in range(pieces):
            across = narrow ^ block
            mine = sum_scr[block]
            other = sum_scr[across].T
            ahead = row + block * size - col - across * size
            real = jnp.where(ahead < 0, mine, jnp.where(ahead > 0, -other, 0.0))
            imag = jnp.where(ahead < 0, other, mine)
            for part in range(per_block):
                at = slice(part * rows, (part + 1) * rows)
                first = 2 * kind * rows
                rows_scr[block * per_block + part, first : first + rows] = real[at]
                rows_scr[block * per_block + part, first + rows : first + 2 * rows] = imag[at]
    for index in range(half):
        own_ref[index] = rows_scr[wide ^ (2 * index)]
        send_ref[index * height : (index + 1) * height] = rows_scr[wide ^ (2 * index + 1)].astype(
            SHORT
        )
    if has_extra:
        send_ref[half * height :] = extra_ref[...]


def expand(here, keep, came, wide_count, extra=None):
    kinds, _, pieces, size, _ = keep.shape
    height = kinds * 2 * pieces * size // wide_count
    half = wide_count // 2
    more = 0 if extra is None else extra.shape[0]
    operands = [here, keep, came] + ([] if extra is None else [extra])
    return call(
        functools.partial(expand_kernel, extra is not None),
        [
            jax.ShapeDtypeStruct((half, height, size), FLOAT),
            jax.ShapeDtypeStruct((half * height + more, size), SHORT),
        ],
        [SMEM_SPEC] + [VMEM_SPEC] * (len(operands) - 1),
        [
            pltpu.VMEM((pieces, size, size), FLOAT),
            pltpu.VMEM((wide_count, height, size), FLOAT),
        ],
    )(*operands)


def spread_kernel(has_extra, own_ref, came_ref, *refs):
    refs = list(refs)
    extra_ref = refs.pop(0) if has_extra else None
    keep_ref, sends = refs[0], refs[1:]
    half, height, _ = own_ref.shape
    keep_ref[...] = own_ref[0] + came_ref[:height].astype(FLOAT)
    for index in range(1, half):
        came = came_ref[index * height : (index + 1) * height].astype(FLOAT)
        sends[index - 1][:height] = (own_ref[index] + came).astype(SHORT)
        if has_extra:
            more = extra_ref.shape[0]
            sends[index - 1][height : height + more] = extra_ref[...]
            sends[index - 1][height + more :] = came_ref[half * height :]


def spread(own, came, extra=None):
    half, height, size = own.shape
    more = 0 if extra is None else 2 * extra.shape[0]
    operands = [own, came] + ([] if extra is None else [extra])
    return call(
        functools.partial(spread_kernel, extra is not None),
        [jax.ShapeDtypeStruct((height, size), FLOAT)]
        + [jax.ShapeDtypeStruct((height + more, size), SHORT)] * (half - 1),
        [VMEM_SPEC] * len(operands),
    )(*operands)


def total_kernel(sources, *refs):
    own_ref, came, rest = refs[0], refs[1 : 1 + sources], refs[1 + sources :]
    out_ref = rest[-1]
    height = own_ref.shape[0]
    total = own_ref[...]
    for ref in came:
        total = total + ref[:height].astype(FLOAT)
    out_ref[:height] = total.astype(SHORT)
    if len(rest) > 1:
        out_ref[height:] = rest[0][...]


def total(own, came, behind=None):
    height, size = own.shape
    more = 0 if behind is None else behind.shape[0]
    operands = [own, *came] + ([] if behind is None else [behind])
    return call(
        functools.partial(total_kernel, len(came)),
        jax.ShapeDtypeStruct((height + more, size), SHORT),
        [VMEM_SPEC] * len(operands),
    )(*operands)


def finish_kernel(order, here_ref, list_ref, *refs):
    pieces = len(order)
    row_refs = refs[:pieces]
    pair_ref, last_refs = refs[pieces], refs[pieces + 1 : -5]
    elem_ref, prod_ref, rows_scr, left_scr, right_scr = refs[-5:]
    narrow, wide = here_ref[0], here_ref[1]
    slots, _, rows, total = elem_ref.shape
    size = row_refs[0].shape[1]
    share = pair_ref.shape[0] // 2
    cols = pair_ref.shape[1] // 2
    height = row_refs[0].shape[0]
    mine = wide * rows // size
    for position, ref in zip(order, row_refs):
        rows_scr[position] = ref[...].reshape(slots, 2 * rows, size)
    for slot in range(slots):
        kind = list_ref[slot]
        for block in range(pieces):
            piece = rows_scr[narrow ^ block ^ mine, kind]
            at = slice(block * size, (block + 1) * size)
            for r in range(2):
                part = piece[r * rows : (r + 1) * rows]
                elem_ref[slot, r, :, at] = part.astype(FLOAT)
                left_scr[
                    slot * rows : (slot + 1) * rows,
                    r * total + block * size : r * total + (block + 1) * size,
                ] = part
    held = [pair_ref[...]]
    held += [ref[ref.shape[0] - 2 * share :, :] for ref in last_refs]
    for index, values in enumerate(held):
        for low in range(2):
            block = values[low * share : (low + 1) * share]
            turned = jnp.concatenate([-block[:, cols:], block[:, :cols]], 1)
            owner = wide ^ (2 * index + low)
            right_scr[0, owner] = block
            right_scr[1, owner] = turned
    right = right_scr[...].reshape(2 * total, 2 * cols)
    product = jnp.dot(left_scr[...], right, preferred_element_type=FLOAT)
    for slot in range(slots):
        for r in range(2):
            prod_ref[slot, r] = product[
                slot * rows : (slot + 1) * rows, r * cols : (r + 1) * cols
            ]


def finish(here, directions, order, rows, pair, last):
    pieces = len(rows)
    slots = directions.shape[0]
    height, size = rows[0].shape
    row_count = height // (2 * slots)
    share, cols = pair.shape[0] // 2, pair.shape[1] // 2
    total = pieces * size
    operands = [*rows, pair, *last]
    return call(
        functools.partial(finish_kernel, order),
        [
            jax.ShapeDtypeStruct((slots, 2, row_count, total), FLOAT),
            jax.ShapeDtypeStruct((slots, 2, row_count, cols), FLOAT),
        ],
        [SMEM_SPEC, SMEM_SPEC] + [VMEM_SPEC] * len(operands),
        [
            pltpu.VMEM((pieces, slots, 2 * row_count, size), SHORT),
            pltpu.VMEM((slots * row_count, 2 * total), SHORT),
            pltpu.VMEM((2, total // share, share, 2 * cols), SHORT),
        ],
    )(here, directions, *operands)


def on_device(vectors, links, directions, peram):
    planes = vectors.shape[3]
    length = vectors.shape[4]
    wide_count = lax.axis_size("wide")
    narrow_count = lax.axis_size("narrow")
    norm = 1.0 / math.sqrt(12.0 * planes * wide_count * length * narrow_count)
    here = jnp.stack([lax.axis_index("narrow"), lax.axis_index("wide")]).astype(jnp.int32)
    link_rows = links.reshape(-1, length)
    pair = jnp.concatenate([peram[0], peram[1]], 1)

    vec, first, edge = split_vectors(vectors)
    plane_halo = from_behind(first, "wide", -1)
    edge_halo = from_behind(edge, "narrow", -1)
    every = tuple(range(planes))
    part = functools.partial(
        direction_part, norm=norm, pieces=narrow_count, here=here, links=link_rows, vec=vec
    )

    def over_narrow(parts, tie=None):
        keep, send = halve(*[(k[None], swap(s, "narrow", 1)[None]) for k, s in parts])
        if tie is not None:
            _, tie = lax.optimization_barrier((keep, tie))
        for stage in range(1, narrow_count.bit_length() - 1):
            came = swap(send, "narrow", 1 << stage)
            if keep.shape[1] > 1:
                keep, send = halve((keep, came))
        return keep, came, tie

    def over_wide(own, send, extra=None):
        came = swap(send, "wide", 1)
        own, *sends = spread(own, came, extra)
        return own, came, [swap(x, "wide", 2 * (i + 1)) for i, x in enumerate(sends)]

    third = part(2, every)
    second = part(1, every, halo=edge_halo)
    inner = part(0, every[:-1], more="first")
    keep, came, plane_halo = over_narrow([second, third], plane_halo)
    early, near, far = over_wide(*expand(here, keep, came, wide_count, pair), pair)
    whole = part(0, every[-1:], halo=plane_halo, more=inner)
    keep, came, _ = over_narrow([whole])
    late, _, rest = over_wide(*expand(here, keep, came, wide_count))
    pairs = jnp.concatenate([pair, near[near.shape[0] - pair.shape[0] :]], 0)

    rows = [total(late, rest, total(early, far))]
    order = [0]
    for stage in reversed(range(narrow_count.bit_length() - 1)):
        rows = rows + [swap(x, "narrow", 1 << stage) for x in rows]
        order = order + [o ^ (1 << stage) for o in order]
    return tuple(finish(here, directions, order, rows, pairs, far))


def solution(mesh):
    placed = (
        P("grp", None, None, "wide", "narrow"),
        P("grp", None, None, None, "wide", "narrow"),
        P(),
        P("grp", "wide", "narrow"),
    )
    return jax.shard_map(
        on_device,
        mesh=mesh,
        in_specs=placed,
        out_specs=(P("grp", None, "wide", None), P("grp", None, "wide", "narrow")),
        check_vma=False,
    )
```

```python
import functools
import math

import jax
import jax.numpy as jnp
from jax import lax
from jax.experimental import pallas as pl
from jax.experimental.pallas import tpu as pltpu
from jax.sharding import PartitionSpec as P

LZ = 16
COMP = 6
VMEM_BYTES = 16 * 1024 * 1024
FLOAT = jnp.float32
SHORT = jnp.bfloat16

VMEM_SPEC = pl.BlockSpec(memory_space=pltpu.VMEM)


def call(kernel, out_shape, in_specs, scratch=()):
    return pl.pallas_call(
        kernel,
        out_shape=out_shape,
        in_specs=in_specs,
        out_specs=jax.tree.map(lambda _: VMEM_SPEC, out_shape),
        scratch_shapes=list(scratch),
        compiler_params=pltpu.CompilerParams(vmem_limit_bytes=VMEM_BYTES),
        cost_estimate=pl.CostEstimate(flops=1, bytes_accessed=1, transcendentals=0),
    )


def from_behind(x, axis, by):
    length = lax.axis_size(axis)
    return lax.ppermute(x, axis, [(i, (i + by) % length) for i in range(length)])


def swap(x, axis, mask):
    length = lax.axis_size(axis)
    return lax.ppermute(x, axis, [(i, i ^ mask) for i in range(length)])


def front_kernel(planes, x_ref, first_ref, wide_scr):
    count = first_ref.shape[0]
    length = x_ref.shape[1]
    wide_scr[...] = x_ref[...].astype(FLOAT)
    for comp in range(COMP):
        values = wide_scr[pl.ds(comp * planes, count, stride=COMP * planes), :]
        first_ref[:, comp * length : (comp + 1) * length] = values.astype(SHORT)


def split_kernel(planes, x_ref, all_ref, edge_ref, wide_scr):
    count = all_ref.shape[0]
    length = x_ref.shape[1]
    per_tile = length // LZ
    wide_scr[...] = x_ref[...].astype(FLOAT)
    lane = lax.broadcasted_iota(jnp.int32, (count, length), 1)
    tiles = [jnp.zeros((count, length), FLOAT)] * (edge_ref.shape[1] // length)
    for plane in range(planes):
        for comp in range(COMP):
            values = wide_scr[pl.ds(comp * planes + plane, count, stride=COMP * planes), :]
            at = (plane * COMP + comp) * length
            all_ref[:, at : at + length] = values.astype(SHORT)
            tile, slot = divmod(plane * COMP + comp, per_tile)
            moved = values if slot == 0 else pltpu.roll(values, slot * LZ, 1)
            tiles[tile] = jnp.where(lane // LZ == slot, moved, tiles[tile])
    for tile, values in enumerate(tiles):
        edge_ref[:, tile * length : (tile + 1) * length] = values.astype(SHORT)


def by_rows(kernel, flat, count, planes, widths, block):
    rows = COMP * planes
    length = flat.shape[1]
    return pl.pallas_call(
        functools.partial(kernel, planes),
        grid=(count // block,),
        out_shape=[jax.ShapeDtypeStruct((count, width), SHORT) for width in widths],
        in_specs=[pl.BlockSpec((block * rows, length), lambda i: (i, 0))],
        out_specs=[pl.BlockSpec((block, width), lambda i: (i, 0)) for width in widths],
        scratch_shapes=[pltpu.VMEM((block * rows, length), FLOAT)],
        compiler_params=pltpu.CompilerParams(vmem_limit_bytes=VMEM_BYTES),
        cost_estimate=pl.CostEstimate(flops=1, bytes_accessed=1, transcendentals=0),
    )(flat)


def split_vectors(vectors):
    count, _, _, planes, length = vectors.shape
    flat = vectors.reshape(-1, length)
    edge_tiles = -(-COMP * planes // (length // LZ))
    (first,) = by_rows(front_kernel, flat, count, planes, [COMP * length], 64)
    _, flat = lax.optimization_barrier((first, flat))
    widths = [COMP * planes * length, edge_tiles * length]
    vec, edge = by_rows(split_kernel, flat, count, planes, widths, 256)
    return vec, first, edge


def times_transposed(left, right):
    return lax.dot_general(left, right, (((1,), (1,)), ((), ())), preferred_element_type=FLOAT)


def direction_kernel(direction, chosen, planes, norm, has_more, has_halo, *refs):
    links_ref, vec_ref = refs[:2]
    rest = list(refs[2:])
    halo_ref = rest.pop(0) if has_halo else None
    more_ref = rest.pop(0) if has_more is True else None
    if has_more == "first":
        whole_ref, fwd_scr, rot_scr = rest
        packed = whole_ref
    else:
        keep_ref, send_ref, fwd_scr, rot_scr, packed = rest
    count = vec_ref.shape[0]
    length = links_ref.shape[1]
    part = 3 * length
    per_tile = length // LZ
    group = 16
    lane = lax.broadcasted_iota(jnp.int32, (group, length), 1)

    def ahead(rows, plane, comp):
        at = (plane * COMP + comp) * length
        if direction == 0:
            if plane + 1 < planes:
                return vec_ref[rows, at + COMP * length : at + (COMP + 1) * length].astype(FLOAT)
            return halo_ref[rows, comp * length : (comp + 1) * length].astype(FLOAT)
        values = vec_ref[rows, at : at + length].astype(FLOAT)
        if direction == 1:
            tile, slot = divmod(plane * COMP + comp, per_tile)
            edge = halo_ref[rows, tile * length : (tile + 1) * length].astype(FLOAT)
            shift = length - LZ - slot * LZ
            edge = edge if shift == 0 else pltpu.roll(edge, shift, 1)
            return jnp.where(lane < length - LZ, pltpu.roll(values, length - LZ, 1), edge)
        return jnp.where(
            lane % LZ == LZ - 1, pltpu.roll(values, LZ - 1, 1), pltpu.roll(values, length - 1, 1)
        )

    for position, plane in enumerate(chosen):
        base = position * COMP * length

        def link(r, a, b):
            row = (((direction * 2 + r) * 3 + a) * 3 + b) * planes + plane
            return links_ref[row : row + 1, :]

        matrix = [[[link(r, a, b) for b in range(3)] for a in range(3)] for r in range(2)]

        def step(index, carry):
            rows = pl.ds(pl.multiple_of(index * group, group), group)
            real = [ahead(rows, plane, b) for b in range(3)]
            imag = [ahead(rows, plane, 3 + b) for b in range(3)]
            for a in range(3):
                out_real = sum(
                    matrix[0][a][b] * real[b] - matrix[1][a][b] * imag[b] for b in range(3)
                )
                out_imag = sum(
                    matrix[0][a][b] * imag[b] + matrix[1][a][b] * real[b] for b in range(3)
                )
                low_real = out_real.astype(SHORT)
                low_imag = out_imag.astype(SHORT)
                at = base + a * length
                fwd_scr[rows, at : at + length] = low_real
                fwd_scr[rows, at + part : at + part + length] = low_imag
                rot_scr[rows, at : at + length] = low_imag
                rot_scr[rows, at + part : at + part + length] = -low_real
            return carry

        lax.fori_loop(0, count // group, step, 0, unroll=8)

    here = lax.axis_index("narrow")
    pieces = packed.shape[0]
    size = packed.shape[2]
    tile = min(256, count)
    first = chosen[0] * COMP * length
    depth = len(chosen) * COMP * length
    row = lax.broadcasted_iota(jnp.int32, (tile, tile), 0)
    col = lax.broadcasted_iota(jnp.int32, (tile, tile), 1)

    def vec(i):
        return vec_ref[i * tile : (i + 1) * tile, first : first + depth]

    def fwd(i):
        return fwd_scr[i * tile : (i + 1) * tile, :]

    def rot(i):
        return rot_scr[i * tile : (i + 1) * tile, :]

    for i in range(count // tile):
        for j in range(count // tile):
            if i < j:
                value = times_transposed(vec(i), fwd(j)) - times_transposed(fwd(i), vec(j))
            elif i > j:
                value = times_transposed(vec(i), rot(j)) + times_transposed(rot(i), vec(j))
            else:
                real = times_transposed(vec(i), fwd(i))
                imag = times_transposed(vec(i), rot(i))
                other = jnp.where(row > col, -real, imag)
                value = jnp.where(row < col, real, imag) + other.T
            value = value * norm
            for p in range(tile // size):
                for q in range(tile // size):
                    block_row = i * (tile // size) + p
                    block_col = j * (tile // size) + q
                    slot = here ^ (block_row ^ block_col)
                    block = value[p * size : (p + 1) * size, q * size : (q + 1) * size]
                    if more_ref is not None:
                        block = block + more_ref[slot, block_row]
                    packed[slot, block_row] = block
    if has_more != "first":
        for piece in range(pieces // 2):
            keep_ref[piece] = packed[2 * piece]
            send_ref[piece] = packed[2 * piece + 1].astype(SHORT)


def direction_part(direction, chosen, norm, pieces, links, vec, halo=None, more=None):
    planes = vec.shape[1] // (COMP * links.shape[1])
    count = vec.shape[0]
    size = count // pieces
    depth = len(chosen) * COMP * links.shape[1]
    whole = jax.ShapeDtypeStruct((pieces, pieces, size, size), FLOAT)
    if more == "first":
        out_shape = whole
    else:
        half = (pieces // 2, pieces, size, size)
        out_shape = [jax.ShapeDtypeStruct(half, FLOAT), jax.ShapeDtypeStruct(half, SHORT)]
    scratch = [pltpu.VMEM((count, depth), SHORT)] * 2
    if more != "first":
        scratch.append(pltpu.VMEM(whole.shape, FLOAT))
    operands = [links, vec]
    if halo is not None:
        operands.append(halo)
    has_more = more if more == "first" else more is not None
    if has_more is True:
        operands.append(more)
    return call(
        functools.partial(
            direction_kernel, direction, chosen, planes, norm, has_more, halo is not None
        ),
        out_shape,
        [VMEM_SPEC] * len(operands),
        scratch,
    )(*operands)


def halve_kernel(sources, *refs):
    keep_ref, send_ref = refs[-2:]
    kind = 0
    for source in range(sources):
        held, came = refs[2 * source], refs[2 * source + 1]
        for k in range(held.shape[0]):
            for piece in range(held.shape[1] // 2):
                even, odd = 2 * piece, 2 * piece + 1
                keep_ref[kind, piece] = held[k, even] + came[k, even].astype(FLOAT)
                send_ref[kind, piece] = (held[k, odd] + came[k, odd].astype(FLOAT)).astype(SHORT)
            kind += 1


def halve(*pairs):
    shape = pairs[0][0].shape
    shape = (sum(held.shape[0] for held, _ in pairs), shape[1] // 2) + shape[2:]
    return call(
        functools.partial(halve_kernel, len(pairs)),
        [jax.ShapeDtypeStruct(shape, FLOAT), jax.ShapeDtypeStruct(shape, SHORT)],
        [VMEM_SPEC] * (2 * len(pairs)),
    )(*[x for pair in pairs for x in pair])


def expand_kernel(has_extra, keep_ref, came_ref, *refs):
    refs = list(refs)
    extra_ref = refs.pop(0) if has_extra else None
    own_ref, send_ref, sum_scr, rows_scr = refs
    narrow, wide = lax.axis_index("narrow"), lax.axis_index("wide")
    kinds, _, pieces, size, _ = keep_ref.shape
    half, height, _ = own_ref.shape
    rows = height // (2 * kinds)
    per_block = size // rows
    row = lax.broadcasted_iota(jnp.int32, (size, size), 0)
    col = lax.broadcasted_iota(jnp.int32, (size, size), 1)
    for kind in range(kinds):
        sum_scr[...] = keep_ref[kind, 0] + came_ref[kind, 0].astype(FLOAT)
        for block in range(pieces):
            across = narrow ^ block
            mine = sum_scr[block]
            other = sum_scr[across].T
            ahead = row + block * size - col - across * size
            real = jnp.where(ahead < 0, mine, jnp.where(ahead > 0, -other, 0.0))
            imag = jnp.where(ahead < 0, other, mine)
            for part in range(per_block):
                at = slice(part * rows, (part + 1) * rows)
                first = 2 * kind * rows
                rows_scr[block * per_block + part, first : first + rows] = real[at]
                rows_scr[block * per_block + part, first + rows : first + 2 * rows] = imag[at]
    for index in range(half):
        own_ref[index] = rows_scr[wide ^ (2 * index)]
        send_ref[index * height : (index + 1) * height] = rows_scr[wide ^ (2 * index + 1)].astype(
            SHORT
        )
    if has_extra:
        send_ref[half * height :] = extra_ref[...]


def expand(keep, came, wide_count, extra=None):
    kinds, _, pieces, size, _ = keep.shape
    height = kinds * 2 * pieces * size // wide_count
    half = wide_count // 2
    more = 0 if extra is None else extra.shape[0]
    operands = [keep, came] + ([] if extra is None else [extra])
    return call(
        functools.partial(expand_kernel, extra is not None),
        [
            jax.ShapeDtypeStruct((half, height, size), FLOAT),
            jax.ShapeDtypeStruct((half * height + more, size), SHORT),
        ],
        [VMEM_SPEC] * len(operands),
        [
            pltpu.VMEM((pieces, size, size), FLOAT),
            pltpu.VMEM((wide_count, height, size), FLOAT),
        ],
    )(*operands)


def spread_kernel(has_extra, own_ref, came_ref, *refs):
    refs = list(refs)
    extra_ref = refs.pop(0) if has_extra else None
    keep_ref, sends = refs[0], refs[1:]
    half, height, _ = own_ref.shape
    keep_ref[...] = own_ref[0] + came_ref[:height].astype(FLOAT)
    for index in range(1, half):
        came = came_ref[index * height : (index + 1) * height].astype(FLOAT)
        sends[index - 1][:height] = (own_ref[index] + came).astype(SHORT)
        if has_extra:
            more = extra_ref.shape[0]
            sends[index - 1][height : height + more] = extra_ref[...]
            sends[index - 1][height + more :] = came_ref[half * height :]


def spread(own, came, extra=None):
    half, height, size = own.shape
    more = 0 if extra is None else 2 * extra.shape[0]
    operands = [own, came] + ([] if extra is None else [extra])
    return call(
        functools.partial(spread_kernel, extra is not None),
        [jax.ShapeDtypeStruct((height, size), FLOAT)]
        + [jax.ShapeDtypeStruct((height + more, size), SHORT)] * (half - 1),
        [VMEM_SPEC] * len(operands),
    )(*operands)


def total_kernel(sources, *refs):
    own_ref, came, rest = refs[0], refs[1 : 1 + sources], refs[1 + sources :]
    out_ref = rest[-1]
    height = own_ref.shape[0]
    total = own_ref[...]
    for ref in came:
        total = total + ref[:height].astype(FLOAT)
    out_ref[:height] = total.astype(SHORT)
    if len(rest) > 1:
        out_ref[height:] = rest[0][...]


def total(own, came, behind=None):
    height, size = own.shape
    more = 0 if behind is None else behind.shape[0]
    operands = [own, *came] + ([] if behind is None else [behind])
    return call(
        functools.partial(total_kernel, len(came)),
        jax.ShapeDtypeStruct((height + more, size), SHORT),
        [VMEM_SPEC] * len(operands),
    )(*operands)


def finish_kernel(order, list_ref, *refs):
    pieces = len(order)
    row_refs = refs[:pieces]
    pair_ref, last_refs = refs[pieces], refs[pieces + 1 : -5]
    elem_ref, prod_ref, rows_scr, left_scr, right_scr = refs[-5:]
    narrow, wide = lax.axis_index("narrow"), lax.axis_index("wide")
    slots, _, rows, total = elem_ref.shape
    size = row_refs[0].shape[1]
    share = pair_ref.shape[0] // 2
    cols = pair_ref.shape[1] // 2
    height = row_refs[0].shape[0]
    mine = wide * rows // size
    for position, ref in zip(order, row_refs):
        rows_scr[position] = ref[...].reshape(slots, 2 * rows, size)
    for block in range(pieces):
        piece = rows_scr[narrow ^ block ^ mine].astype(FLOAT)
        at = slice(block * size, (block + 1) * size)
        for slot in range(slots):
            chosen = piece[0]
            for kind in range(1, slots):
                chosen = jnp.where(list_ref[slot] == kind, piece[kind], chosen)
            for r in range(2):
                part = chosen[r * rows : (r + 1) * rows]
                elem_ref[slot, r, :, at] = part
                left_scr[
                    slot * rows : (slot + 1) * rows,
                    r * total + block * size : r * total + (block + 1) * size,
                ] = part.astype(SHORT)
    held = [pair_ref[...]]
    held += [ref[ref.shape[0] - 2 * share :, :] for ref in last_refs]
    for index, values in enumerate(held):
        for low in range(2):
            block = values[low * share : (low + 1) * share]
            turned = jnp.concatenate([-block[:, cols:], block[:, :cols]], 1)
            owner = wide ^ (2 * index + low)
            right_scr[0, owner] = block
            right_scr[1, owner] = turned
    right = right_scr[...].reshape(2 * total, 2 * cols)
    product = jnp.dot(left_scr[...], right, preferred_element_type=FLOAT)
    for slot in range(slots):
        for r in range(2):
            prod_ref[slot, r] = product[
                slot * rows : (slot + 1) * rows, r * cols : (r + 1) * cols
            ]


def finish(directions, order, rows, pair, last):
    pieces = len(rows)
    slots = directions.shape[0]
    height, size = rows[0].shape
    row_count = height // (2 * slots)
    share, cols = pair.shape[0] // 2, pair.shape[1] // 2
    total = pieces * size
    operands = [*rows, pair, *last]
    return call(
        functools.partial(finish_kernel, order),
        [
            jax.ShapeDtypeStruct((slots, 2, row_count, total), FLOAT),
            jax.ShapeDtypeStruct((slots, 2, row_count, cols), FLOAT),
        ],
        [VMEM_SPEC] * (1 + len(operands)),
        [
            pltpu.VMEM((pieces, slots, 2 * row_count, size), SHORT),
            pltpu.VMEM((slots * row_count, 2 * total), SHORT),
            pltpu.VMEM((2, total // share, share, 2 * cols), SHORT),
        ],
    )(jnp.broadcast_to(directions[:, None, None], (slots, 1, size)), *operands)


def on_device(vectors, links, directions, peram):
    planes = vectors.shape[3]
    length = vectors.shape[4]
    wide_count = lax.axis_size("wide")
    narrow_count = lax.axis_size("narrow")
    norm = 1.0 / math.sqrt(12.0 * planes * wide_count * length * narrow_count)
    link_rows = links.reshape(-1, length)
    pair = jnp.concatenate([peram[0], peram[1]], 1)

    vec, first, edge = split_vectors(vectors)
    plane_halo = from_behind(first, "wide", -1)
    edge_halo = from_behind(edge, "narrow", -1)
    every = tuple(range(planes))
    part = functools.partial(
        direction_part, norm=norm, pieces=narrow_count, links=link_rows, vec=vec
    )

    def over_narrow(parts, tie=None):
        keep, send = halve(*[(k[None], swap(s, "narrow", 1)[None]) for k, s in parts])
        if tie is not None:
            _, tie = lax.optimization_barrier((keep, tie))
        for stage in range(1, narrow_count.bit_length() - 1):
            came = swap(send, "narrow", 1 << stage)
            if keep.shape[1] > 1:
                keep, send = halve((keep, came))
        return keep, came, tie

    def over_wide(own, send, extra=None):
        came = swap(send, "wide", 1)
        own, *sends = spread(own, came, extra)
        return own, came, [swap(x, "wide", 2 * (i + 1)) for i, x in enumerate(sends)]

    third = part(2, every)
    second = part(1, every, halo=edge_halo)
    inner = part(0, every[:-1], more="first")
    keep, came, plane_halo = over_narrow([second, third], plane_halo)
    early, near, far = over_wide(*expand(keep, came, wide_count, pair), pair)
    whole = part(0, every[-1:], halo=plane_halo, more=inner)
    keep, came, _ = over_narrow([whole])
    late, _, rest = over_wide(*expand(keep, came, wide_count))
    pairs = jnp.concatenate([pair, near[near.shape[0] - pair.shape[0] :]], 0)

    rows = [total(late, rest, total(early, far))]
    order = [0]
    for stage in reversed(range(narrow_count.bit_length() - 1)):
        rows = rows + [swap(x, "narrow", 1 << stage) for x in rows]
        order = order + [o ^ (1 << stage) for o in order]
    return tuple(finish(directions, order, rows, pairs, far))


def solution(mesh):
    placed = (
        P("grp", None, None, "wide", "narrow"),
        P("grp", None, None, None, "wide", "narrow"),
        P(),
        P("grp", "wide", "narrow"),
    )
    return jax.shard_map(
        on_device,
        mesh=mesh,
        in_specs=placed,
        out_specs=(P("grp", None, "wide", None), P("grp", None, "wide", "narrow")),
        check_vma=False,
    )
```

```python
import functools
import math

import jax
import jax.numpy as jnp
from jax import lax
from jax.experimental import pallas as pl
from jax.experimental.pallas import tpu as pltpu
from jax.sharding import PartitionSpec as P

LZ = 16
COMP = 6
VMEM_BYTES = 16 * 1024 * 1024
FLOAT = jnp.float32
SHORT = jnp.bfloat16

VMEM_SPEC = pl.BlockSpec(memory_space=pltpu.VMEM)


def call(kernel, out_shape, in_specs, scratch=()):
    return pl.pallas_call(
        kernel,
        out_shape=out_shape,
        in_specs=in_specs,
        out_specs=jax.tree.map(lambda _: VMEM_SPEC, out_shape),
        scratch_shapes=list(scratch),
        compiler_params=pltpu.CompilerParams(vmem_limit_bytes=VMEM_BYTES),
        cost_estimate=pl.CostEstimate(flops=1, bytes_accessed=1, transcendentals=0),
    )


def from_behind(x, axis, by):
    length = lax.axis_size(axis)
    return lax.ppermute(x, axis, [(i, (i + by) % length) for i in range(length)])


def swap(x, axis, mask):
    length = lax.axis_size(axis)
    return lax.ppermute(x, axis, [(i, i ^ mask) for i in range(length)])


def front_kernel(planes, x_ref, first_ref, wide_scr):
    count = first_ref.shape[0]
    length = x_ref.shape[1]
    wide_scr[...] = x_ref[...].astype(FLOAT)
    for comp in range(COMP):
        values = wide_scr[pl.ds(comp * planes, count, stride=COMP * planes), :]
        first_ref[:, comp * length : (comp + 1) * length] = values.astype(SHORT)


def split_kernel(planes, x_ref, all_ref, edge_ref, wide_scr):
    count = all_ref.shape[0]
    length = x_ref.shape[1]
    per_tile = length // LZ
    wide_scr[...] = x_ref[...].astype(FLOAT)
    lane = lax.broadcasted_iota(jnp.int32, (count, length), 1)
    tiles = [jnp.zeros((count, length), FLOAT)] * (edge_ref.shape[1] // length)
    for plane in range(planes):
        for comp in range(COMP):
            values = wide_scr[pl.ds(comp * planes + plane, count, stride=COMP * planes), :]
            at = (plane * COMP + comp) * length
            all_ref[:, at : at + length] = values.astype(SHORT)
            tile, slot = divmod(plane * COMP + comp, per_tile)
            moved = values if slot == 0 else pltpu.roll(values, slot * LZ, 1)
            tiles[tile] = jnp.where(lane // LZ == slot, moved, tiles[tile])
    for tile, values in enumerate(tiles):
        edge_ref[:, tile * length : (tile + 1) * length] = values.astype(SHORT)


def by_rows(kernel, flat, count, planes, widths, block):
    rows = COMP * planes
    length = flat.shape[1]
    return pl.pallas_call(
        functools.partial(kernel, planes),
        grid=(count // block,),
        out_shape=[jax.ShapeDtypeStruct((count, width), SHORT) for width in widths],
        in_specs=[pl.BlockSpec((block * rows, length), lambda i: (i, 0))],
        out_specs=[pl.BlockSpec((block, width), lambda i: (i, 0)) for width in widths],
        scratch_shapes=[pltpu.VMEM((block * rows, length), FLOAT)],
        compiler_params=pltpu.CompilerParams(vmem_limit_bytes=VMEM_BYTES),
        cost_estimate=pl.CostEstimate(flops=1, bytes_accessed=1, transcendentals=0),
    )(flat)


def split_vectors(vectors):
    count, _, _, planes, length = vectors.shape
    flat = vectors.reshape(-1, length)
    edge_tiles = -(-COMP * planes // (length // LZ))
    (first,) = by_rows(front_kernel, flat, count, planes, [COMP * length], 64)
    _, flat = lax.optimization_barrier((first, flat))
    widths = [COMP * planes * length, edge_tiles * length]
    vec, edge = by_rows(split_kernel, flat, count, planes, widths, 256)
    return vec, first, edge


def times_transposed(left, right):
    return lax.dot_general(left, right, (((1,), (1,)), ((), ())), preferred_element_type=FLOAT)


def direction_kernel(direction, chosen, planes, norm, has_more, has_halo, *refs):
    links_ref, vec_ref = refs[:2]
    rest = list(refs[2:])
    halo_ref = rest.pop(0) if has_halo else None
    more_ref = rest.pop(0) if has_more is True else None
    if has_more == "first":
        whole_ref, fwd_scr, rot_scr = rest
        packed = whole_ref
    else:
        keep_ref, send_ref, fwd_scr, rot_scr, packed = rest
    count = vec_ref.shape[0]
    length = links_ref.shape[1]
    part = 3 * length
    per_tile = length // LZ
    group = 16
    lane = lax.broadcasted_iota(jnp.int32, (group, length), 1)

    def ahead(rows, plane, comp):
        at = (plane * COMP + comp) * length
        if direction == 0:
            if plane + 1 < planes:
                return vec_ref[rows, at + COMP * length : at + (COMP + 1) * length].astype(FLOAT)
            return halo_ref[rows, comp * length : (comp + 1) * length].astype(FLOAT)
        values = vec_ref[rows, at : at + length].astype(FLOAT)
        if direction == 1:
            tile, slot = divmod(plane * COMP + comp, per_tile)
            edge = halo_ref[rows, tile * length : (tile + 1) * length].astype(FLOAT)
            shift = length - LZ - slot * LZ
            edge = edge if shift == 0 else pltpu.roll(edge, shift, 1)
            return jnp.where(lane < length - LZ, pltpu.roll(values, length - LZ, 1), edge)
        return jnp.where(
            lane % LZ == LZ - 1, pltpu.roll(values, LZ - 1, 1), pltpu.roll(values, length - 1, 1)
        )

    for position, plane in enumerate(chosen):
        base = position * COMP * length

        def link(r, a, b):
            row = (((direction * 2 + r) * 3 + a) * 3 + b) * planes + plane
            return links_ref[row : row + 1, :]

        matrix = [[[link(r, a, b) for b in range(3)] for a in range(3)] for r in range(2)]

        def step(index, carry):
            rows = pl.ds(pl.multiple_of(index * group, group), group)
            real = [ahead(rows, plane, b) for b in range(3)]
            imag = [ahead(rows, plane, 3 + b) for b in range(3)]
            for a in range(3):
                out_real = sum(
                    matrix[0][a][b] * real[b] - matrix[1][a][b] * imag[b] for b in range(3)
                )
                out_imag = sum(
                    matrix[0][a][b] * imag[b] + matrix[1][a][b] * real[b] for b in range(3)
                )
                low_real = out_real.astype(SHORT)
                low_imag = out_imag.astype(SHORT)
                at = base + a * length
                fwd_scr[rows, at : at + length] = low_real
                fwd_scr[rows, at + part : at + part + length] = low_imag
                rot_scr[rows, at : at + length] = low_imag
                rot_scr[rows, at + part : at + part + length] = -low_real
            return carry

        lax.fori_loop(0, count // group, step, 0, unroll=8)

    here = lax.axis_index("narrow")
    pieces = packed.shape[0]
    size = packed.shape[2]
    tile = min(256, count)
    first = chosen[0] * COMP * length
    depth = len(chosen) * COMP * length
    row = lax.broadcasted_iota(jnp.int32, (tile, tile), 0)
    col = lax.broadcasted_iota(jnp.int32, (tile, tile), 1)

    def vec(i):
        return vec_ref[i * tile : (i + 1) * tile, first : first + depth]

    def fwd(i):
        return fwd_scr[i * tile : (i + 1) * tile, :]

    def rot(i):
        return rot_scr[i * tile : (i + 1) * tile, :]

    for i in range(count // tile):
        for j in range(count // tile):
            if i < j:
                value = times_transposed(vec(i), fwd(j)) - times_transposed(fwd(i), vec(j))
            elif i > j:
                value = times_transposed(vec(i), rot(j)) + times_transposed(rot(i), vec(j))
            else:
                real = times_transposed(vec(i), fwd(i))
                imag = times_transposed(vec(i), rot(i))
                other = jnp.where(row > col, -real, imag)
                value = jnp.where(row < col, real, imag) + other.T
            value = value * norm
            for p in range(tile // size):
                for q in range(tile // size):
                    block_row = i * (tile // size) + p
                    block_col = j * (tile // size) + q
                    slot = here ^ (block_row ^ block_col)
                    block = value[p * size : (p + 1) * size, q * size : (q + 1) * size]
                    if more_ref is not None:
                        block = block + more_ref[slot, block_row]
                    packed[slot, block_row] = block
    if has_more != "first":
        for piece in range(pieces // 2):
            keep_ref[piece] = packed[2 * piece]
            send_ref[piece] = packed[2 * piece + 1].astype(SHORT)


def direction_part(direction, chosen, norm, pieces, links, vec, halo=None, more=None):
    planes = vec.shape[1] // (COMP * links.shape[1])
    count = vec.shape[0]
    size = count // pieces
    depth = len(chosen) * COMP * links.shape[1]
    whole = jax.ShapeDtypeStruct((pieces, pieces, size, size), FLOAT)
    if more == "first":
        out_shape = whole
    else:
        half = (pieces // 2, pieces, size, size)
        out_shape = [jax.ShapeDtypeStruct(half, FLOAT), jax.ShapeDtypeStruct(half, SHORT)]
    scratch = [pltpu.VMEM((count, depth), SHORT)] * 2
    if more != "first":
        scratch.append(pltpu.VMEM(whole.shape, FLOAT))
    operands = [links, vec]
    if halo is not None:
        operands.append(halo)
    has_more = more if more == "first" else more is not None
    if has_more is True:
        operands.append(more)
    return call(
        functools.partial(
            direction_kernel, direction, chosen, planes, norm, has_more, halo is not None
        ),
        out_shape,
        [VMEM_SPEC] * len(operands),
        scratch,
    )(*operands)


def halve_kernel(sources, *refs):
    keep_ref, send_ref = refs[-2:]
    kind = 0
    for source in range(sources):
        held, came = refs[2 * source], refs[2 * source + 1]
        for k in range(held.shape[0]):
            for piece in range(held.shape[1] // 2):
                even, odd = 2 * piece, 2 * piece + 1
                keep_ref[kind, piece] = held[k, even] + came[k, even].astype(FLOAT)
                send_ref[kind, piece] = (held[k, odd] + came[k, odd].astype(FLOAT)).astype(SHORT)
            kind += 1


def halve(*pairs):
    shape = pairs[0][0].shape
    shape = (sum(held.shape[0] for held, _ in pairs), shape[1] // 2) + shape[2:]
    return call(
        functools.partial(halve_kernel, len(pairs)),
        [jax.ShapeDtypeStruct(shape, FLOAT), jax.ShapeDtypeStruct(shape, SHORT)],
        [VMEM_SPEC] * (2 * len(pairs)),
    )(*[x for pair in pairs for x in pair])


def expand_kernel(keep_ref, came_ref, own_ref, send_ref, sum_scr, rows_scr):
    narrow, wide = lax.axis_index("narrow"), lax.axis_index("wide")
    kinds, _, pieces, size, _ = keep_ref.shape
    half, height, _ = own_ref.shape
    rows = height // (2 * kinds)
    per_block = size // rows
    row = lax.broadcasted_iota(jnp.int32, (size, size), 0)
    col = lax.broadcasted_iota(jnp.int32, (size, size), 1)
    for kind in range(kinds):
        sum_scr[...] = keep_ref[kind, 0] + came_ref[kind, 0].astype(FLOAT)
        for block in range(pieces):
            across = narrow ^ block
            mine = sum_scr[block]
            other = sum_scr[across].T
            ahead = row + block * size - col - across * size
            real = jnp.where(ahead < 0, mine, jnp.where(ahead > 0, -other, 0.0))
            imag = jnp.where(ahead < 0, other, mine)
            for part in range(per_block):
                at = slice(part * rows, (part + 1) * rows)
                first = 2 * kind * rows
                rows_scr[block * per_block + part, first : first + rows] = real[at]
                rows_scr[block * per_block + part, first + rows : first + 2 * rows] = imag[at]
    for index in range(half):
        own_ref[index] = rows_scr[wide ^ (2 * index)]
        send_ref[index * height : (index + 1) * height] = rows_scr[wide ^ (2 * index + 1)].astype(
            SHORT
        )


def expand(keep, came, wide_count):
    kinds, _, pieces, size, _ = keep.shape
    height = kinds * 2 * pieces * size // wide_count
    half = wide_count // 2
    return call(
        expand_kernel,
        [
            jax.ShapeDtypeStruct((half, height, size), FLOAT),
            jax.ShapeDtypeStruct((half * height, size), SHORT),
        ],
        [VMEM_SPEC] * 2,
        [
            pltpu.VMEM((pieces, size, size), FLOAT),
            pltpu.VMEM((wide_count, height, size), FLOAT),
        ],
    )(keep, came)


def spread_kernel(has_extra, own_ref, came_ref, *refs):
    refs = list(refs)
    extra_ref = refs.pop(0) if has_extra else None
    keep_ref, sends = refs[0], refs[1:]
    half, height, _ = own_ref.shape
    keep_ref[...] = own_ref[0] + came_ref[:height].astype(FLOAT)
    for index in range(1, half):
        came = came_ref[index * height : (index + 1) * height].astype(FLOAT)
        sends[index - 1][:height] = (own_ref[index] + came).astype(SHORT)
        if has_extra:
            sends[index - 1][height:] = extra_ref[...]


def spread(own, came, extra=None):
    half, height, size = own.shape
    more = 0 if extra is None else extra.shape[0]
    operands = [own, came] + ([] if extra is None else [extra])
    return call(
        functools.partial(spread_kernel, extra is not None),
        [jax.ShapeDtypeStruct((height, size), FLOAT)]
        + [jax.ShapeDtypeStruct((height + more, size), SHORT)] * (half - 1),
        [VMEM_SPEC] * len(operands),
    )(*operands)


def total_kernel(sources, *refs):
    own_ref, came, rest = refs[0], refs[1 : 1 + sources], refs[1 + sources :]
    out_ref = rest[-1]
    height = own_ref.shape[0]
    total = own_ref[...]
    for ref in came:
        total = total + ref[:height].astype(FLOAT)
    out_ref[:height] = total.astype(SHORT)
    if len(rest) > 1:
        out_ref[height:] = rest[0][...]


def total(own, came, behind=None):
    height, size = own.shape
    more = 0 if behind is None else behind.shape[0]
    operands = [own, *came] + ([] if behind is None else [behind])
    return call(
        functools.partial(total_kernel, len(came)),
        jax.ShapeDtypeStruct((height + more, size), SHORT),
        [VMEM_SPEC] * len(operands),
    )(*operands)


def finish_kernel(order, list_ref, *refs):
    pieces = len(order)
    row_refs = refs[:pieces]
    held_refs, other_ref = refs[pieces:-6], refs[-6]
    elem_ref, prod_ref, rows_scr, left_scr, right_scr = refs[-5:]
    narrow, wide = lax.axis_index("narrow"), lax.axis_index("wide")
    slots, _, rows, total = elem_ref.shape
    size = row_refs[0].shape[1]
    share, cols = right_scr.shape[2], right_scr.shape[3] // 2
    height = row_refs[0].shape[0]
    mine = wide * rows // size
    for position, ref in zip(order, row_refs):
        rows_scr[position] = ref[...].reshape(slots, 2 * rows, size)
    for block in range(pieces):
        piece = rows_scr[narrow ^ block ^ mine].astype(FLOAT)
        at = slice(block * size, (block + 1) * size)
        for slot in range(slots):
            chosen = piece[0]
            for kind in range(1, slots):
                chosen = jnp.where(list_ref[:, slot : slot + 1] == kind, piece[kind], chosen)
            for r in range(2):
                part = chosen[r * rows : (r + 1) * rows]
                elem_ref[slot, r, :, at] = part
                left_scr[
                    slot * rows : (slot + 1) * rows,
                    r * total + block * size : r * total + (block + 1) * size,
                ] = part.astype(SHORT)
    for index, ref in enumerate(held_refs):
        for low in range(2):
            if low == 0:
                block = ref[ref.shape[0] - share :, :]
            else:
                block = other_ref[index * share : (index + 1) * share]
            owner = wide ^ (2 * index + low)
            right_scr[0, owner] = block
            right_scr[1, owner] = jnp.concatenate([-block[:, cols:], block[:, :cols]], 1)
    right = right_scr[...].reshape(2 * total, 2 * cols)
    product = jnp.dot(left_scr[...], right, preferred_element_type=FLOAT)
    for slot in range(slots):
        for r in range(2):
            prod_ref[slot, r] = product[
                slot * rows : (slot + 1) * rows, r * cols : (r + 1) * cols
            ]


def finish(directions, order, rows, held, other):
    pieces = len(rows)
    slots = directions.shape[0]
    height, size = rows[0].shape
    row_count = height // (2 * slots)
    share, cols = held[0].shape[0], held[0].shape[1] // 2
    total = pieces * size
    operands = [*rows, *held, other]
    return call(
        functools.partial(finish_kernel, order),
        [
            jax.ShapeDtypeStruct((slots, 2, row_count, total), FLOAT),
            jax.ShapeDtypeStruct((slots, 2, row_count, cols), FLOAT),
        ],
        [VMEM_SPEC] * (1 + len(operands)),
        [
            pltpu.VMEM((pieces, slots, 2 * row_count, size), SHORT),
            pltpu.VMEM((slots * row_count, 2 * total), SHORT),
            pltpu.VMEM((2, total // share, share, 2 * cols), SHORT),
        ],
    )(directions[None], *operands)


def on_device(vectors, links, directions, peram):
    planes = vectors.shape[3]
    length = vectors.shape[4]
    wide_count = lax.axis_size("wide")
    narrow_count = lax.axis_size("narrow")
    norm = 1.0 / math.sqrt(12.0 * planes * wide_count * length * narrow_count)
    link_rows = links.reshape(-1, length)
    pair = jnp.concatenate([peram[0], peram[1]], 1)

    vec, first, edge = split_vectors(vectors)
    plane_halo = from_behind(first, "wide", -1)
    edge_halo = from_behind(edge, "narrow", -1)
    every = tuple(range(planes))
    part = functools.partial(
        direction_part, norm=norm, pieces=narrow_count, links=link_rows, vec=vec
    )

    def over_narrow(parts, tie=None):
        keep, send = halve(*[(k[None], swap(s, "narrow", 1)[None]) for k, s in parts])
        if tie is not None:
            _, tie = lax.optimization_barrier((keep, tie))
        for stage in range(1, narrow_count.bit_length() - 1):
            came = swap(send, "narrow", 1 << stage)
            if keep.shape[1] > 1:
                keep, send = halve((keep, came))
        return keep, came, tie

    def over_wide(own, send, extra=None):
        came = swap(send, "wide", 1)
        own, *sends = spread(own, came, extra)
        return own, came, [swap(x, "wide", 2 * (i + 1)) for i, x in enumerate(sends)]

    third = part(2, every)
    second = part(1, every, halo=edge_halo)
    keep, came, plane_halo = over_narrow([second, third], plane_halo)
    calm, _ = lax.optimization_barrier((vec, keep))
    inner = part(0, every[:-1], more="first", vec=calm)
    early, _, far = over_wide(*expand(keep, came, wide_count), pair)
    whole = part(0, every[-1:], halo=plane_halo, more=inner)
    keep, came, _ = over_narrow([whole])
    late, _, rest = over_wide(*expand(keep, came, wide_count))
    held = [pair] + [x[x.shape[0] - pair.shape[0] :] for x in far]
    other = swap(jnp.concatenate(held, 0), "wide", 1)

    rows = [total(late, rest, total(early, far))]
    order = [0]
    for stage in reversed(range(narrow_count.bit_length() - 1)):
        came = [swap(x, "narrow", 1 << stage) for x in rows]
        if stage > 0:
            came, other = lax.optimization_barrier((came, other))
        rows = rows + came
        order = order + [o ^ (1 << stage) for o in order]
    return tuple(finish(directions, order, rows, held, other))


def solution(mesh):
    placed = (
        P("grp", None, None, "wide", "narrow"),
        P("grp", None, None, None, "wide", "narrow"),
        P(),
        P("grp", "wide", "narrow"),
    )
    return jax.shard_map(
        on_device,
        mesh=mesh,
        in_specs=placed,
        out_specs=(P("grp", None, "wide", None), P("grp", None, "wide", "narrow")),
        check_vma=False,
    )
```

```python
import functools
import math

import jax
import jax.numpy as jnp
from jax import lax
from jax.experimental import pallas as pl
from jax.experimental.pallas import tpu as pltpu
from jax.sharding import PartitionSpec as P

LZ = 16
COMP = 6
VMEM_BYTES = 16 * 1024 * 1024
FLOAT = jnp.float32
SHORT = jnp.bfloat16

VMEM_SPEC = pl.BlockSpec(memory_space=pltpu.VMEM)


def call(kernel, out_shape, in_specs, scratch=()):
    return pl.pallas_call(
        kernel,
        out_shape=out_shape,
        in_specs=in_specs,
        out_specs=jax.tree.map(lambda _: VMEM_SPEC, out_shape),
        scratch_shapes=list(scratch),
        compiler_params=pltpu.CompilerParams(vmem_limit_bytes=VMEM_BYTES),
        cost_estimate=pl.CostEstimate(flops=1, bytes_accessed=1, transcendentals=0),
    )


def from_behind(x, axis, by):
    length = lax.axis_size(axis)
    return lax.ppermute(x, axis, [(i, (i + by) % length) for i in range(length)])


def swap(x, axis, mask):
    length = lax.axis_size(axis)
    return lax.ppermute(x, axis, [(i, i ^ mask) for i in range(length)])


def front_kernel(planes, x_ref, first_ref, wide_scr):
    count = first_ref.shape[0]
    length = x_ref.shape[1]
    wide_scr[...] = x_ref[...].astype(FLOAT)
    for comp in range(COMP):
        values = wide_scr[pl.ds(comp * planes, count, stride=COMP * planes), :]
        first_ref[:, comp * length : (comp + 1) * length] = values.astype(SHORT)


def split_kernel(planes, x_ref, all_ref, edge_ref, wide_scr):
    count = all_ref.shape[0]
    length = x_ref.shape[1]
    per_tile = length // LZ
    wide_scr[...] = x_ref[...].astype(FLOAT)
    lane = lax.broadcasted_iota(jnp.int32, (count, length), 1)
    tiles = [jnp.zeros((count, length), FLOAT)] * (edge_ref.shape[1] // length)
    for plane in range(planes):
        for comp in range(COMP):
            values = wide_scr[pl.ds(comp * planes + plane, count, stride=COMP * planes), :]
            at = (plane * COMP + comp) * length
            all_ref[:, at : at + length] = values.astype(SHORT)
            tile, slot = divmod(plane * COMP + comp, per_tile)
            moved = values if slot == 0 else pltpu.roll(values, slot * LZ, 1)
            tiles[tile] = jnp.where(lane // LZ == slot, moved, tiles[tile])
    for tile, values in enumerate(tiles):
        edge_ref[:, tile * length : (tile + 1) * length] = values.astype(SHORT)


def by_rows(kernel, flat, count, planes, widths, block):
    rows = COMP * planes
    length = flat.shape[1]
    return pl.pallas_call(
        functools.partial(kernel, planes),
        grid=(count // block,),
        out_shape=[jax.ShapeDtypeStruct((count, width), SHORT) for width in widths],
        in_specs=[pl.BlockSpec((block * rows, length), lambda i: (i, 0))],
        out_specs=[pl.BlockSpec((block, width), lambda i: (i, 0)) for width in widths],
        scratch_shapes=[pltpu.VMEM((block * rows, length), FLOAT)],
        compiler_params=pltpu.CompilerParams(vmem_limit_bytes=VMEM_BYTES),
        cost_estimate=pl.CostEstimate(flops=1, bytes_accessed=1, transcendentals=0),
    )(flat)


def split_vectors(vectors):
    count, _, _, planes, length = vectors.shape
    flat = vectors.reshape(-1, length)
    edge_tiles = -(-COMP * planes // (length // LZ))
    (first,) = by_rows(front_kernel, flat, count, planes, [COMP * length], 64)
    _, flat = lax.optimization_barrier((first, flat))
    widths = [COMP * planes * length, edge_tiles * length]
    vec, edge = by_rows(split_kernel, flat, count, planes, widths, 256)
    return vec, first, edge


def times_transposed(left, right):
    return lax.dot_general(left, right, (((1,), (1,)), ((), ())), preferred_element_type=FLOAT)


def direction_kernel(direction, chosen, planes, norm, has_more, has_halo, *refs):
    links_ref, vec_ref = refs[:2]
    rest = list(refs[2:])
    halo_ref = rest.pop(0) if has_halo else None
    more_ref = rest.pop(0) if has_more is True else None
    if has_more == "first":
        whole_ref, fwd_scr, rot_scr = rest
        packed = whole_ref
    else:
        keep_ref, send_ref, fwd_scr, rot_scr, packed = rest
    count = vec_ref.shape[0]
    length = links_ref.shape[1]
    part = 3 * length
    per_tile = length // LZ
    group = 16
    lane = lax.broadcasted_iota(jnp.int32, (group, length), 1)

    def ahead(rows, plane, comp):
        at = (plane * COMP + comp) * length
        if direction == 0:
            if plane + 1 < planes:
                return vec_ref[rows, at + COMP * length : at + (COMP + 1) * length].astype(FLOAT)
            return halo_ref[rows, comp * length : (comp + 1) * length].astype(FLOAT)
        values = vec_ref[rows, at : at + length].astype(FLOAT)
        if direction == 1:
            tile, slot = divmod(plane * COMP + comp, per_tile)
            edge = halo_ref[rows, tile * length : (tile + 1) * length].astype(FLOAT)
            shift = length - LZ - slot * LZ
            edge = edge if shift == 0 else pltpu.roll(edge, shift, 1)
            return jnp.where(lane < length - LZ, pltpu.roll(values, length - LZ, 1), edge)
        return jnp.where(
            lane % LZ == LZ - 1, pltpu.roll(values, LZ - 1, 1), pltpu.roll(values, length - 1, 1)
        )

    for position, plane in enumerate(chosen):
        base = position * COMP * length

        def link(r, a, b):
            row = (((direction * 2 + r) * 3 + a) * 3 + b) * planes + plane
            return links_ref[row : row + 1, :]

        matrix = [[[link(r, a, b) for b in range(3)] for a in range(3)] for r in range(2)]

        def step(index, carry):
            rows = pl.ds(pl.multiple_of(index * group, group), group)
            real = [ahead(rows, plane, b) for b in range(3)]
            imag = [ahead(rows, plane, 3 + b) for b in range(3)]
            for a in range(3):
                out_real = sum(
                    matrix[0][a][b] * real[b] - matrix[1][a][b] * imag[b] for b in range(3)
                )
                out_imag = sum(
                    matrix[0][a][b] * imag[b] + matrix[1][a][b] * real[b] for b in range(3)
                )
                low_real = out_real.astype(SHORT)
                low_imag = out_imag.astype(SHORT)
                at = base + a * length
                fwd_scr[rows, at : at + length] = low_real
                fwd_scr[rows, at + part : at + part + length] = low_imag
                rot_scr[rows, at : at + length] = low_imag
                rot_scr[rows, at + part : at + part + length] = -low_real
            return carry

        lax.fori_loop(0, count // group, step, 0, unroll=16)

    here = lax.axis_index("narrow")
    pieces = packed.shape[0]
    size = packed.shape[2]
    tile = min(256, count)
    first = chosen[0] * COMP * length
    depth = len(chosen) * COMP * length
    row = lax.broadcasted_iota(jnp.int32, (tile, tile), 0)
    col = lax.broadcasted_iota(jnp.int32, (tile, tile), 1)

    def vec(i):
        return vec_ref[i * tile : (i + 1) * tile, first : first + depth]

    def fwd(i):
        return fwd_scr[i * tile : (i + 1) * tile, :]

    def rot(i):
        return rot_scr[i * tile : (i + 1) * tile, :]

    for i in range(count // tile):
        for j in range(count // tile):
            if i < j:
                value = times_transposed(vec(i), fwd(j)) - times_transposed(fwd(i), vec(j))
            elif i > j:
                value = times_transposed(vec(i), rot(j)) + times_transposed(rot(i), vec(j))
            else:
                real = times_transposed(vec(i), fwd(i))
                imag = times_transposed(vec(i), rot(i))
                other = jnp.where(row > col, -real, imag)
                value = jnp.where(row < col, real, imag) + other.T
            value = value * norm
            for p in range(tile // size):
                for q in range(tile // size):
                    block_row = i * (tile // size) + p
                    block_col = j * (tile // size) + q
                    slot = here ^ (block_row ^ block_col)
                    block = value[p * size : (p + 1) * size, q * size : (q + 1) * size]
                    if more_ref is not None:
                        block = block + more_ref[slot, block_row]
                    packed[slot, block_row] = block
    if has_more != "first":
        for piece in range(pieces // 2):
            keep_ref[piece] = packed[2 * piece]
            send_ref[piece] = packed[2 * piece + 1].astype(SHORT)


def direction_part(direction, chosen, norm, pieces, links, vec, halo=None, more=None):
    planes = vec.shape[1] // (COMP * links.shape[1])
    count = vec.shape[0]
    size = count // pieces
    depth = len(chosen) * COMP * links.shape[1]
    whole = jax.ShapeDtypeStruct((pieces, pieces, size, size), FLOAT)
    if more == "first":
        out_shape = whole
    else:
        half = (pieces // 2, pieces, size, size)
        out_shape = [jax.ShapeDtypeStruct(half, FLOAT), jax.ShapeDtypeStruct(half, SHORT)]
    scratch = [pltpu.VMEM((count, depth), SHORT)] * 2
    if more != "first":
        scratch.append(pltpu.VMEM(whole.shape, FLOAT))
    operands = [links, vec]
    if halo is not None:
        operands.append(halo)
    has_more = more if more == "first" else more is not None
    if has_more is True:
        operands.append(more)
    return call(
        functools.partial(
            direction_kernel, direction, chosen, planes, norm, has_more, halo is not None
        ),
        out_shape,
        [VMEM_SPEC] * len(operands),
        scratch,
    )(*operands)


def halve_kernel(sources, *refs):
    keep_ref, send_ref = refs[-2:]
    kind = 0
    for source in range(sources):
        held, came = refs[2 * source], refs[2 * source + 1]
        for k in range(held.shape[0]):
            for piece in range(held.shape[1] // 2):
                even, odd = 2 * piece, 2 * piece + 1
                keep_ref[kind, piece] = held[k, even] + came[k, even].astype(FLOAT)
                send_ref[kind, piece] = (held[k, odd] + came[k, odd].astype(FLOAT)).astype(SHORT)
            kind += 1


def halve(*pairs):
    shape = pairs[0][0].shape
    shape = (sum(held.shape[0] for held, _ in pairs), shape[1] // 2) + shape[2:]
    return call(
        functools.partial(halve_kernel, len(pairs)),
        [jax.ShapeDtypeStruct(shape, FLOAT), jax.ShapeDtypeStruct(shape, SHORT)],
        [VMEM_SPEC] * (2 * len(pairs)),
    )(*[x for pair in pairs for x in pair])


def expand_kernel(keep_ref, came_ref, own_ref, send_ref, sum_scr, rows_scr):
    narrow, wide = lax.axis_index("narrow"), lax.axis_index("wide")
    kinds, _, pieces, size, _ = keep_ref.shape
    half, height, _ = own_ref.shape
    rows = height // (2 * kinds)
    per_block = size // rows
    row = lax.broadcasted_iota(jnp.int32, (size, size), 0)
    col = lax.broadcasted_iota(jnp.int32, (size, size), 1)
    for kind in range(kinds):
        sum_scr[...] = keep_ref[kind, 0] + came_ref[kind, 0].astype(FLOAT)
        for block in range(pieces):
            across = narrow ^ block
            mine = sum_scr[block]
            other = sum_scr[across].T
            ahead = row + block * size - col - across * size
            real = jnp.where(ahead < 0, mine, jnp.where(ahead > 0, -other, 0.0))
            imag = jnp.where(ahead < 0, other, mine)
            for part in range(per_block):
                at = slice(part * rows, (part + 1) * rows)
                first = 2 * kind * rows
                rows_scr[block * per_block + part, first : first + rows] = real[at]
                rows_scr[block * per_block + part, first + rows : first + 2 * rows] = imag[at]
    for index in range(half):
        own_ref[index] = rows_scr[wide ^ (2 * index)]
        send_ref[index * height : (index + 1) * height] = rows_scr[wide ^ (2 * index + 1)].astype(
            SHORT
        )


def expand(keep, came, wide_count):
    kinds, _, pieces, size, _ = keep.shape
    height = kinds * 2 * pieces * size // wide_count
    half = wide_count // 2
    return call(
        expand_kernel,
        [
            jax.ShapeDtypeStruct((half, height, size), FLOAT),
            jax.ShapeDtypeStruct((half * height, size), SHORT),
        ],
        [VMEM_SPEC] * 2,
        [
            pltpu.VMEM((pieces, size, size), FLOAT),
            pltpu.VMEM((wide_count, height, size), FLOAT),
        ],
    )(keep, came)


def spread_kernel(has_extra, own_ref, came_ref, *refs):
    refs = list(refs)
    extra_ref = refs.pop(0) if has_extra else None
    keep_ref, sends = refs[0], refs[1:]
    half, height, _ = own_ref.shape
    keep_ref[...] = own_ref[0] + came_ref[:height].astype(FLOAT)
    for index in range(1, half):
        came = came_ref[index * height : (index + 1) * height].astype(FLOAT)
        sends[index - 1][:height] = (own_ref[index] + came).astype(SHORT)
        if has_extra:
            sends[index - 1][height:] = extra_ref[...]


def spread(own, came, extra=None):
    half, height, size = own.shape
    more = 0 if extra is None else extra.shape[0]
    operands = [own, came] + ([] if extra is None else [extra])
    return call(
        functools.partial(spread_kernel, extra is not None),
        [jax.ShapeDtypeStruct((height, size), FLOAT)]
        + [jax.ShapeDtypeStruct((height + more, size), SHORT)] * (half - 1),
        [VMEM_SPEC] * len(operands),
    )(*operands)


def total_kernel(sources, *refs):
    own_ref, came, rest = refs[0], refs[1 : 1 + sources], refs[1 + sources :]
    out_ref = rest[-1]
    height = own_ref.shape[0]
    total = own_ref[...]
    for ref in came:
        total = total + ref[:height].astype(FLOAT)
    out_ref[:height] = total.astype(SHORT)
    if len(rest) > 1:
        out_ref[height:] = rest[0][...]


def total(own, came, behind=None):
    height, size = own.shape
    more = 0 if behind is None else behind.shape[0]
    operands = [own, *came] + ([] if behind is None else [behind])
    return call(
        functools.partial(total_kernel, len(came)),
        jax.ShapeDtypeStruct((height + more, size), SHORT),
        [VMEM_SPEC] * len(operands),
    )(*operands)


def finish_kernel(order, list_ref, *refs):
    pieces = len(order)
    row_refs = refs[:pieces]
    held_refs, other_ref = refs[pieces:-6], refs[-6]
    elem_ref, prod_ref, rows_scr, left_scr, right_scr = refs[-5:]
    narrow, wide = lax.axis_index("narrow"), lax.axis_index("wide")
    slots, _, rows, total = elem_ref.shape
    size = row_refs[0].shape[1]
    share, cols = right_scr.shape[2], right_scr.shape[3] // 2
    height = row_refs[0].shape[0]
    mine = wide * rows // size
    for position, ref in zip(order, row_refs):
        rows_scr[position] = ref[...].reshape(slots, 2 * rows, size)
    for block in range(pieces):
        piece = rows_scr[narrow ^ block ^ mine].astype(FLOAT)
        at = slice(block * size, (block + 1) * size)
        for slot in range(slots):
            chosen = piece[0]
            for kind in range(1, slots):
                chosen = jnp.where(list_ref[:, slot : slot + 1] == kind, piece[kind], chosen)
            for r in range(2):
                part = chosen[r * rows : (r + 1) * rows]
                elem_ref[slot, r, :, at] = part
                left_scr[
                    slot * rows : (slot + 1) * rows,
                    r * total + block * size : r * total + (block + 1) * size,
                ] = part.astype(SHORT)
    for index, ref in enumerate(held_refs):
        for low in range(2):
            if low == 0:
                block = ref[ref.shape[0] - share :, :]
            else:
                block = other_ref[index * share : (index + 1) * share]
            owner = wide ^ (2 * index + low)
            right_scr[0, owner] = block
            right_scr[1, owner] = jnp.concatenate([-block[:, cols:], block[:, :cols]], 1)
    right = right_scr[...].reshape(2 * total, 2 * cols)
    product = jnp.dot(left_scr[...], right, preferred_element_type=FLOAT)
    for slot in range(slots):
        for r in range(2):
            prod_ref[slot, r] = product[
                slot * rows : (slot + 1) * rows, r * cols : (r + 1) * cols
            ]


def finish(directions, order, rows, held, other):
    pieces = len(rows)
    slots = directions.shape[0]
    height, size = rows[0].shape
    row_count = height // (2 * slots)
    share, cols = held[0].shape[0], held[0].shape[1] // 2
    total = pieces * size
    operands = [*rows, *held, other]
    return call(
        functools.partial(finish_kernel, order),
        [
            jax.ShapeDtypeStruct((slots, 2, row_count, total), FLOAT),
            jax.ShapeDtypeStruct((slots, 2, row_count, cols), FLOAT),
        ],
        [VMEM_SPEC] * (1 + len(operands)),
        [
            pltpu.VMEM((pieces, slots, 2 * row_count, size), SHORT),
            pltpu.VMEM((slots * row_count, 2 * total), SHORT),
            pltpu.VMEM((2, total // share, share, 2 * cols), SHORT),
        ],
    )(directions[None], *operands)


def on_device(vectors, links, directions, peram):
    planes = vectors.shape[3]
    length = vectors.shape[4]
    wide_count = lax.axis_size("wide")
    narrow_count = lax.axis_size("narrow")
    norm = 1.0 / math.sqrt(12.0 * planes * wide_count * length * narrow_count)
    link_rows = links.reshape(-1, length)
    pair = jnp.concatenate([peram[0], peram[1]], 1)

    vec, first, edge = split_vectors(vectors)
    plane_halo = from_behind(first, "wide", -1)
    edge_halo = from_behind(edge, "narrow", -1)
    every = tuple(range(planes))
    part = functools.partial(
        direction_part, norm=norm, pieces=narrow_count, links=link_rows, vec=vec
    )

    def over_narrow(parts, tie=None):
        keep, send = halve(*[(k[None], swap(s, "narrow", 1)[None]) for k, s in parts])
        if tie is not None:
            _, tie = lax.optimization_barrier((keep, tie))
        for stage in range(1, narrow_count.bit_length() - 1):
            came = swap(send, "narrow", 1 << stage)
            if keep.shape[1] > 1:
                keep, send = halve((keep, came))
        return keep, came, tie

    def over_wide(own, send, extra=None):
        came = swap(send, "wide", 1)
        own, *sends = spread(own, came, extra)
        return own, came, [swap(x, "wide", 2 * (i + 1)) for i, x in enumerate(sends)]

    third = part(2, every)
    second = part(1, every, halo=edge_halo)
    keep, came, plane_halo = over_narrow([second, third], plane_halo)
    calm, _ = lax.optimization_barrier((vec, keep))
    inner = part(0, every[:-1], more="first", vec=calm)
    early, _, far = over_wide(*expand(keep, came, wide_count), pair)
    whole = part(0, every[-1:], halo=plane_halo, more=inner)
    keep, came, _ = over_narrow([whole])
    late, _, rest = over_wide(*expand(keep, came, wide_count))
    held = [pair] + [x[x.shape[0] - pair.shape[0] :] for x in far]
    other = swap(jnp.concatenate(held, 0), "wide", 1)

    rows = [total(late, rest, total(early, far))]
    order = [0]
    for stage in reversed(range(narrow_count.bit_length() - 1)):
        came = [swap(x, "narrow", 1 << stage) for x in rows]
        if stage > 0:
            came, other = lax.optimization_barrier((came, other))
        rows = rows + came
        order = order + [o ^ (1 << stage) for o in order]
    return tuple(finish(directions, order, rows, held, other))


def solution(mesh):
    placed = (
        P("grp", None, None, "wide", "narrow"),
        P("grp", None, None, None, "wide", "narrow"),
        P(),
        P("grp", "wide", "narrow"),
    )
    return jax.shard_map(
        on_device,
        mesh=mesh,
        in_specs=placed,
        out_specs=(P("grp", None, "wide", None), P("grp", None, "wide", "narrow")),
        check_vma=False,
    )
```
